512 devices in a mesh: dp: 4 (over x), tm: 8 (over y, core), rows: 16 (over z).
Axes of the slice: x: 4, y: 4, z: 16, core: 2. Of those that a mesh axis runs over, the one named last changes fastest.
Arguments:
- clips: bfloat16 [4, 16, 64, 64, 256], P('dp', 'tm', 'rows'), may hold values from -6 to 6
- segment_ids: int32 [4, 16], P('dp'), may hold values from 0 to 3, never falling along the last dimension, each value on 1 to 8 neighbouring positions
- spatial_weight: bfloat16 [2, 9, 256, 256], replicated, may hold values from -0.125 to 0.125
- temporal_weight: bfloat16 [2, 3, 256, 256], replicated, may hold values from -0.21875 to 0.21875
- upstream: bfloat16 [4, 16, 64, 64, 256], P('dp', 'tm', 'rows'), may hold values from -6 to 6
Outputs:
- input_grad: bfloat16 [4, 16, 64, 64, 256], P('dp', 'tm', 'rows')
- features: bfloat16 [4, 16, 64, 64, 256], P('dp', 'tm', 'rows')
- temporal_grad: float32 [1536, 256], P('rows')
The draws below stay inside these ranges and needn't reach their ends.
Inputs may be any that keep to these rules, and one draw needn't show every extreme that they name: `segment_ids`: frame numbers of packed clips in each row never fall; each packed clip has 1 to 8 frames and one has exactly 8.
All inputs are finite; a program needn't handle non-finite values.
Results may differ from the reference program's by a relative error of at most 0.015.
Values may be sent and summed in bfloat16 or wider, within the bound.
A program may use at most 64 MiB of HBM per device.

```python
import math
import jax
import jax.numpy as jnp
import numpy as np

C = 256
COLS = 64
LAYERS = 2
BATCH = 4
FRAMES = 16
HEIGHT = 64
SEGS = 4
SEG_MOST = 8


def block_levels(key, dims, cuts, least, high):
    loudness = 1.0
    for position, blocks in cuts:
        steps = jax.random.uniform(jax.random.fold_in(jax.random.fold_in(key, 6), position), (blocks,), jnp.float32, least / len(cuts), high / len(cuts))
        loudness = loudness * jnp.repeat(jnp.exp(steps), dims[position] // blocks).reshape((-1,) + (1,) * (len(dims) - 1 - position))
    return loudness


def split_up(count, total, bound, lean):
    loads = [(1 << 20) // math.isqrt(rank ** lean) + 1 for rank in range(2, count + 1)]
    surplus, holding = total - bound - (count - 1), [1] * (count - 1)
    while surplus > 0:
        movable = [i for i in range(count - 1) if holding[i] < bound]
        pool, remaining = sum([loads[i] for i in movable]), surplus
        for i in movable:
            extra = min(bound - holding[i], max(1, remaining * loads[i] // pool), surplus)
            holding[i] = holding[i] + extra
            surplus = surplus - extra
    return np.array([bound] + holding)


def ragged(rng, number_of, total, reach, lean):
    if number_of == 2:
        one = jax.random.randint(rng, (), max(1, total - reach), min(reach, total - 1) + 1)
        return jnp.stack([one, total - one])
    lengths = jnp.asarray(split_up(number_of, total, reach, lean), jnp.int32)
    couples = (number_of - 1) // 2
    giver, sink = lengths[1:1 + 2 * couples:2], lengths[2:2 + 2 * couples:2]
    slack = jnp.minimum(giver - 1, reach - sink)
    shifted = jax.random.randint(jax.random.fold_in(rng, 1), (couples,), 0, 1 << 20) % (slack + 1)
    lengths = lengths.at[1:1 + 2 * couples:2].set(giver - shifted).at[2:2 + 2 * couples:2].set(sink + shifted)
    return lengths[jax.random.permutation(jax.random.fold_in(rng, 2), number_of)]


def noise(key, shape, width, bound, split=(), kind=jnp.bfloat16):
    array = width * jax.random.normal(key, shape, jnp.float32)
    if split:
        array = array * block_levels(key, shape, split, -0.22, 0.18)
    return jnp.clip(array, -bound, bound).astype(kind)


def setup_inputs(seed: int = 0) -> dict:
    key_list = jax.random.split(jax.random.key(seed), 6)
    clips = noise(key_list[0], (BATCH, FRAMES, HEIGHT, COLS, C), 1.0, 6.0, ((0, 4), (1, 8), (2, 16)))
    segment_ids = jax.vmap(lambda own: jnp.searchsorted(jnp.cumsum(ragged(own, SEGS, FRAMES, SEG_MOST, 0)), jnp.arange(FRAMES), side="right"))(jax.random.split(key_list[1], BATCH)).reshape((BATCH, FRAMES)).astype(jnp.int32)
    spatial_weight = noise(key_list[2], (LAYERS, 9, C, C), (9 * C) ** -0.5, 0.125)
    temporal_weight = noise(key_list[3], (LAYERS, 3, C, C), (3 * C) ** -0.5, 0.21875)
    upstream = noise(key_list[4], (BATCH, FRAMES, HEIGHT, COLS, C), 1.0, 6.0, ((0, 4), (1, 8), (2, 16)))
    return dict(clips=clips, segment_ids=segment_ids, spatial_weight=spatial_weight, temporal_weight=temporal_weight, upstream=upstream)


def silu_slope(values):
    sigma = jax.nn.sigmoid(values)
    return sigma * (1.0 + values * (1.0 - sigma))


def frame_masks(segments):
    frame_total = segments.shape[0]
    positions = jnp.arange(frame_total, dtype=jnp.int32)
    masks = []
    for offset in range(3):
        earlier = jnp.concatenate([jnp.full((offset,), -1, jnp.int32), segments[:frame_total - offset]])
        masks.append((positions >= offset) & (earlier == segments))
    return masks


def spatial(inputs, weights, flipped):
    height = inputs.shape[1]
    columns = inputs.shape[2]
    channels = inputs.shape[3]
    padded = jnp.pad(inputs, ((0, 0), (1, 1), (1, 1), (0, 0)))
    accumulated = jnp.zeros(inputs.shape, jnp.float32)
    for tap_index in range(9):
        row_off = tap_index // 3
        col_off = tap_index % 3
        matrix = weights[tap_index]
        if flipped:
            row_off = 2 - row_off
            col_off = 2 - col_off
            matrix = matrix.T
        window = padded[:, row_off:row_off + height, col_off:col_off + columns, :]
        product = jnp.dot(window.reshape(-1, channels), matrix, preferred_element_type=jnp.float32)
        accumulated = accumulated + product.reshape(inputs.shape)
    return accumulated


def delayed(values, offset):
    frame_total = values.shape[0]
    filler = jnp.zeros((offset,) + values.shape[1:], values.dtype)
    return jnp.concatenate([filler, values[:frame_total - offset]], axis=0)


def temporal(activated, weights, masks):
    channels = activated.shape[-1]
    accumulated = jnp.zeros(activated.shape, jnp.float32)
    for offset in range(3):
        source = delayed(activated, offset)
        product = jnp.dot(source.reshape(-1, channels), weights[offset], preferred_element_type=jnp.float32)
        accumulated = accumulated + jnp.where(masks[offset][:, None, None, None], product.reshape(activated.shape), 0.0)
    return accumulated


def temporal_back(activated, grad_out, weights, masks):
    channels = activated.shape[-1]
    frame_total = activated.shape[0]
    grad_act = jnp.zeros(activated.shape, jnp.float32)
    pieces = []
    for offset in range(3):
        masked = jnp.where(masks[offset][:, None, None, None], grad_out, jnp.zeros_like(grad_out))
        filler = jnp.zeros((offset,) + grad_out.shape[1:], grad_out.dtype)
        lifted = jnp.concatenate([masked[offset:], filler], axis=0)
        product = jnp.dot(lifted.reshape(-1, channels), weights[offset].T, preferred_element_type=jnp.float32)
        grad_act = grad_act + product.reshape(activated.shape)
        source = delayed(activated, offset)
        pieces.append(jnp.dot(source.reshape(-1, channels).T, masked.reshape(-1, channels), preferred_element_type=jnp.float32))
    return grad_act, jnp.stack(pieces)


def reference(clips, segment_ids, spatial_weight, temporal_weight, upstream):
    grads_all = jnp.zeros((LAYERS, 3, C, C), jnp.float32)
    grad_list = []
    feature_list = []
    for clip_index in range(BATCH):
        masks = frame_masks(segment_ids[clip_index])
        layer_in = clips[clip_index]
        saved = []
        for layer_index in range(LAYERS):
            spatial_sum = spatial(layer_in, spatial_weight[layer_index], False)
            activated = jax.nn.silu(spatial_sum).astype(jnp.bfloat16)
            temporal_sum = temporal(activated, temporal_weight[layer_index], masks)
            saved.append((spatial_sum, activated))
            layer_in = (layer_in.astype(jnp.float32) + temporal_sum).astype(jnp.bfloat16)
        feature_list.append(layer_in)
        grad_in = upstream[clip_index]
        for layer_index in reversed(range(LAYERS)):
            spatial_sum, activated = saved[layer_index]
            grad_act, weight_grad = temporal_back(activated, grad_in, temporal_weight[layer_index], masks)
            grads_all = grads_all.at[layer_index].add(weight_grad)
            grad_pre = (grad_act * silu_slope(spatial_sum)).astype(jnp.bfloat16)
            back = spatial(grad_pre, spatial_weight[layer_index], True)
            grad_in = (grad_in.astype(jnp.float32) + back).astype(jnp.bfloat16)
        grad_list.append(grad_in)
    return jnp.stack(grad_list), jnp.stack(feature_list), grads_all.reshape(LAYERS * 3 * C, C)
```

```python
import jax
import jax.numpy as jnp
from jax import lax
from jax.experimental import pallas as pl
from jax.experimental.pallas import tpu as pltpu
from jax.sharding import PartitionSpec as P


def with_halo(cells, sides, width):
    for axis, dim in sides:
        count = lax.axis_size(axis)
        ends = count - 1
        head = lax.slice_in_dim(cells, 0, width, axis=dim)
        tail = lax.slice_in_dim(cells, cells.shape[dim] - width, cells.shape[dim], axis=dim)
        cells = jnp.concatenate(
            [
                lax.ppermute(tail, axis, [(i, (i + 1) % count) for i in range(ends)]),
                cells,
                lax.ppermute(head, axis, [((i + 1) % count, i) for i in range(ends)]),
            ],
            axis=dim,
        )
    return cells


def from_behind(value, axis, steps):
    count = lax.axis_size(axis)
    first, last = (max(0, -steps), min(count, count - steps))
    return lax.ppermute(value, axis, [(source, source + steps) for source in range(first, last)])


def silu_slope(values):
    sigma = jax.nn.sigmoid(values)
    return sigma * (1.0 + values * (1.0 - sigma))


def frame_masks(segments, first_frame, frame_count):
    frame_total = segments.shape[0]
    positions = jnp.arange(frame_total, dtype=jnp.int32)
    global_pos = first_frame + jnp.arange(frame_count, dtype=jnp.int32)

    def lookup(frame_pos):
        matches = positions[None, :] == frame_pos[:, None]
        return jnp.sum(jnp.where(matches, segments[None, :], 0), axis=1)

    own_ids = lookup(global_pos)
    masks = []
    for offset in range(3):
        source = global_pos - offset
        masks.append((source >= 0) & (lookup(source) == own_ids))
    return masks


def spatial_local(padded, weights, flipped):
    height = padded.shape[2] - 2
    columns = padded.shape[3]
    channels = padded.shape[4]
    wide = jnp.pad(padded, ((0, 0), (0, 0), (0, 0), (1, 1), (0, 0)))
    out_shape = padded.shape[:2] + (height, columns, channels)
    accumulated = jnp.zeros(out_shape, jnp.float32)
    for tap_index in range(9):
        row_off = tap_index // 3
        col_off = tap_index % 3
        matrix = weights[tap_index]
        if flipped:
            row_off = 2 - row_off
            col_off = 2 - col_off
            matrix = matrix.T
        window = wide[:, :, row_off : row_off + height, col_off : col_off + columns, :]
        product = jnp.dot(window.reshape(-1, channels), matrix, preferred_element_type=jnp.float32)
        accumulated = accumulated + product.reshape(out_shape)
    return accumulated


def forward_layer(layer_in, space_weights, time_weights, own_masks):
    frames_dev = layer_in.shape[1]
    channels = layer_in.shape[4]
    padded = with_halo(layer_in, (("rows", 2),), 1)
    spatial_sum = spatial_local(padded, space_weights, False)
    activated = jax.nn.silu(spatial_sum).astype(jnp.bfloat16)
    prior = from_behind(activated, "tm", 1)
    joined = jnp.concatenate([prior, activated], axis=1)
    accumulated = jnp.zeros(activated.shape, jnp.float32)
    for offset in range(3):
        source = joined[:, frames_dev - offset : 2 * frames_dev - offset]
        product = jnp.dot(
            source.reshape(-1, channels), time_weights[offset], preferred_element_type=jnp.float32
        )
        accumulated = accumulated + jnp.where(
            own_masks[offset][None, :, None, None, None], product.reshape(activated.shape), 0.0
        )
    layer_out = (layer_in.astype(jnp.float32) + accumulated).astype(jnp.bfloat16)
    return (layer_out, spatial_sum, joined)


def backward_layer(
    grad_in, spatial_sum, joined, space_weights, time_weights, own_masks, next_masks
):
    frames_dev = grad_in.shape[1]
    channels = grad_in.shape[4]
    later = from_behind(grad_in, "tm", -1)
    extended = jnp.concatenate([grad_in, later], axis=1)
    grad_act = jnp.zeros(grad_in.shape, jnp.float32)
    pieces = []
    for offset in range(3):
        both_masks = jnp.concatenate([own_masks[offset], next_masks[offset]])
        masked = jnp.where(
            both_masks[None, :, None, None, None], extended, jnp.zeros_like(extended)
        )
        lifted = masked[:, offset : offset + frames_dev]
        product = jnp.dot(
            lifted.reshape(-1, channels), time_weights[offset].T, preferred_element_type=jnp.float32
        )
        grad_act = grad_act + product.reshape(grad_in.shape)
        source = joined[:, frames_dev - offset : 2 * frames_dev - offset].reshape(-1, channels)
        own_part = masked[:, :frames_dev].reshape(-1, channels)
        pieces.append(
            lax.dot_general(
                source, own_part, (((0,), (0,)), ((), ())), preferred_element_type=jnp.float32
            )
        )
    grad_pre = (grad_act * silu_slope(spatial_sum)).astype(jnp.bfloat16)
    padded = with_halo(grad_pre, (("rows", 2),), 1)
    back = spatial_local(padded, space_weights, True)
    grad_out = (grad_in.astype(jnp.float32) + back).astype(jnp.bfloat16)
    return (grad_out, jnp.stack(pieces))

XS, YS, CORES, ZS = 4, 4, 2, 16
CHIPS = XS * YS
PLANE = CHIPS * CORES
PIECE = 6
HALF = 128


def sum_kernel(part_ref, out_ref, arranged, send_pair, recv_pair, send_plane, recv_plane, send_z, recv_z,
               total, recv_all, sems):
    x = lax.axis_index("dp")
    t = lax.axis_index("tm")
    z = lax.axis_index("rows")
    core = t % CORES
    chip = x * YS + t // CORES
    place = x * (YS * CORES) + t

    def plane_id(other):
        return {"dp": other // (YS * CORES), "tm": other % (YS * CORES)}

    def chip_id(other):
        return {"dp": other // YS, "tm": (other % YS) * CORES + core}

    barrier = pltpu.get_barrier_semaphore()

    @pl.loop(1, PLANE)
    def _(step):
        pl.semaphore_signal(barrier, inc=1, device_id=plane_id((place + step) % PLANE))

    @pl.loop(1, ZS)
    def _(step):
        pl.semaphore_signal(barrier, inc=1, device_id={"rows": (z + step) % ZS})

    @pl.loop(0, XS)
    def _(high):
        for block in range(ZS):
            rows = part_ref[pl.ds(pl.multiple_of(96 * block + PIECE * YS * high, 8), PIECE * YS), :]
            for low in range(YS):
                arranged[high * YS + low, PIECE * block : PIECE * (block + 1), :] = rows[
                    PIECE * low : PIECE * (low + 1)
                ]

    @pl.loop(0, CHIPS)
    def _(group):
        rows = arranged[group]
        other = jnp.where(core == 0, rows[:, HALF:], rows[:, :HALF])
        send_pair[group] = other.astype(jnp.bfloat16)

    pl.semaphore_wait(barrier, PLANE - 1 + ZS - 1)
    pair = pltpu.make_async_remote_copy(
        src_ref=send_pair, dst_ref=recv_pair, send_sem=sems.at[0], recv_sem=sems.at[1],
        device_id={"tm": t + 1 - 2 * core},
    )
    pair.start()
    pair.wait()

    @pl.loop(0, CHIPS)
    def _(group):
        rows = arranged[group]
        own = jnp.where(core == 0, rows[:, :HALF], rows[:, HALF:])
        send_plane[group] = (own + recv_pair[group].astype(jnp.float32)).astype(jnp.bfloat16)

    @pl.loop(1, CHIPS)
    def _(step):
        other = (chip + step) % CHIPS
        pltpu.make_async_remote_copy(
            src_ref=send_plane.at[other], dst_ref=recv_plane.at[chip], send_sem=sems.at[2], recv_sem=sems.at[3],
            device_id=chip_id(other),
        ).start()

    recv_plane[chip] = send_plane[chip]
    both = pltpu.make_async_remote_copy(
        src_ref=send_plane.at[pl.ds(0, CHIPS - 1)], dst_ref=recv_plane.at[pl.ds(0, CHIPS - 1)],
        send_sem=sems.at[2], recv_sem=sems.at[3], device_id=chip_id((chip + 1) % CHIPS),
    )
    both.wait()
    summed = recv_plane[0].astype(jnp.float32)
    for group in range(1, CHIPS):
        summed = summed + recv_plane[group].astype(jnp.float32)
    for block in range(ZS):
        send_z[block, :PIECE, :] = summed[PIECE * block : PIECE * (block + 1), :]
        send_z[block, PIECE:, :] = jnp.zeros((8 - PIECE, HALF), jnp.float32)

    @pl.loop(1, ZS)
    def _(step):
        other = (z + step) % ZS
        pltpu.make_async_remote_copy(
            src_ref=send_z.at[other], dst_ref=recv_z.at[z], send_sem=sems.at[4], recv_sem=sems.at[5],
            device_id={"rows": other},
        ).start()

    recv_z[z] = send_z[z]
    pltpu.make_async_remote_copy(
        src_ref=send_z.at[pl.ds(0, ZS - 1)], dst_ref=recv_z.at[pl.ds(0, ZS - 1)],
        send_sem=sems.at[4], recv_sem=sems.at[5], device_id={"rows": (z + 1) % ZS},
    ).wait()
    final = recv_z[0]
    for block in range(1, ZS):
        final = final + recv_z[block]
    total[...] = final

    @pl.loop(1, PLANE)
    def _(step):
        pltpu.make_async_remote_copy(
            src_ref=total, dst_ref=recv_all.at[place], send_sem=sems.at[6], recv_sem=sems.at[7],
            device_id=plane_id((place + step) % PLANE),
        ).start()

    recv_all[place] = final
    pltpu.make_async_remote_copy(
        src_ref=recv_all.at[pl.ds(0, PLANE - 1)], dst_ref=recv_all.at[pl.ds(0, PLANE - 1)],
        send_sem=sems.at[6], recv_sem=sems.at[7], device_id=plane_id((place + 1) % PLANE),
    ).wait()
    for group in range(CHIPS):
        for half in range(CORES):
            out_ref[PIECE * group : PIECE * (group + 1), HALF * half : HALF * (half + 1)] = recv_all[
                group * CORES + half, :PIECE, :
            ]


def summed_gradient(partial_grad):
    rows, columns = partial_grad.shape
    deep = PIECE * ZS
    return pl.pallas_call(
        sum_kernel,
        out_shape=jax.ShapeDtypeStruct((rows // ZS, columns), jnp.float32),
        in_specs=[pl.BlockSpec(memory_space=pltpu.VMEM)],
        out_specs=pl.BlockSpec(memory_space=pltpu.VMEM),
        scratch_shapes=[
            pltpu.VMEM((CHIPS, deep, columns), jnp.float32),
            pltpu.VMEM((CHIPS, deep, HALF), jnp.bfloat16),
            pltpu.VMEM((CHIPS, deep, HALF), jnp.bfloat16),
            pltpu.VMEM((CHIPS, deep, HALF), jnp.bfloat16),
            pltpu.VMEM((CHIPS, deep, HALF), jnp.bfloat16),
            pltpu.VMEM((ZS, 8, HALF), jnp.float32),
            pltpu.VMEM((ZS, 8, HALF), jnp.float32),
            pltpu.VMEM((8, HALF), jnp.float32),
            pltpu.VMEM((PLANE, 8, HALF), jnp.float32),
            pltpu.SemaphoreType.DMA((8,)),
        ],
        compiler_params=pltpu.CompilerParams(
            collective_id=0, has_side_effects=True, vmem_limit_bytes=40 * 1024 * 1024
        ),
    )(partial_grad)


def local(clips, segment_ids, spatial_weight, temporal_weight, upstream):
    frames_dev = clips.shape[1]
    segments = segment_ids[0]
    chain_pos = lax.axis_index("tm")
    own_masks = frame_masks(segments, chain_pos * frames_dev, frames_dev)
    next_masks = frame_masks(segments, (chain_pos + 1) * frames_dev, frames_dev)
    layer_count = spatial_weight.shape[0]
    layer_in = clips
    saved = []
    for layer_index in range(layer_count):
        layer_in, spatial_sum, joined = forward_layer(
            layer_in, spatial_weight[layer_index], temporal_weight[layer_index], own_masks
        )
        saved.append((spatial_sum, joined))
    grad_in = upstream
    layer_grads = [None] * layer_count
    for layer_index in reversed(range(layer_count)):
        spatial_sum, joined = saved[layer_index]
        grad_in, weight_grad = backward_layer(
            grad_in,
            spatial_sum,
            joined,
            spatial_weight[layer_index],
            temporal_weight[layer_index],
            own_masks,
            next_masks,
        )
        flat_grad = weight_grad.reshape(-1, weight_grad.shape[-1])
        layer_grads[layer_index] = flat_grad
    partial_grad = jnp.concatenate(layer_grads, axis=0)
    result = summed_gradient(partial_grad)
    return (grad_in, layer_in, result)


def solution(mesh):
    return jax.shard_map(
        local,
        mesh=mesh,
        in_specs=(
            P("dp", "tm", "rows", None, None),
            P("dp", None),
            P(),
            P(),
            P("dp", "tm", "rows", None, None),
        ),
        out_specs=(
            P("dp", "tm", "rows", None, None),
            P("dp", "tm", "rows", None, None),
            P("rows", None),
        ),
        check_vma=False,
    )
```

```python
import jax
import jax.numpy as jnp
from jax import lax
from jax.experimental import pallas as pl
from jax.experimental.pallas import tpu as pltpu
from jax.sharding import PartitionSpec as P

XS, YS, CORES, ZS = 4, 4, 2, 16
TS = YS * CORES
CHIPS = XS * YS
PLANE = CHIPS * CORES
PIECE = 6
HALF = 128
C = 256
COLS = 64
ROWS = 4
OWN = 2
CELLS = OWN * ROWS * COLS
FRAMES = TS * OWN
BF, F32 = jnp.bfloat16, jnp.float32
NT = (((1,), (1,)), ((), ()))


def mm(left, right):
    return jnp.dot(left, right, preferred_element_type=F32)


def mm_nt(left, right):
    return lax.dot_general(left, right, NT, preferred_element_type=F32)


def rows_of(padded, first):
    return padded[:, first : first + ROWS].reshape(CELLS, C)


def shifted(values, by):
    column = lax.broadcasted_iota(jnp.int32, values.shape, 0) % COLS
    edge = 0 if by == 1 else COLS - 1
    return jnp.where(column == edge, 0.0, pltpu.roll(values, by % CELLS, 0))


def spatial(padded, weights):
    sums = []
    for kx in range(3):
        left = jnp.concatenate([rows_of(padded, ky) for ky in range(3)], axis=1)
        right = jnp.concatenate([weights[ky, kx] for ky in range(3)], axis=0)
        sums.append(mm(left, right))
    return shifted(sums[0], 1) + sums[1] + shifted(sums[2], -1)


def spatial_back(padded, weights):
    sums = []
    for kx in range(3):
        total = None
        for ky in range(3):
            part = mm_nt(rows_of(padded, 2 - ky), weights[ky, kx])
            total = part if total is None else total + part
        sums.append(total)
    return shifted(sums[0], -1) + sums[1] + shifted(sums[2], 1)


def kernel(
    seg, clips, space_w, time_w, upstream,
    grad_out, feat_out, weight_out,
    ws, wt, xh, acts, slopes, grads, dh, dact, turned, part, feat, gin,
    arranged, send_pair, recv_pair, send_plane, recv_plane, send_z, recv_z, total, recv_all, result,
    load, halo_s, halo_r, time_s, time_r, sums, store,
):
    x = lax.axis_index("dp")
    t = lax.axis_index("tm")
    z = lax.axis_index("rows")
    core = t % CORES
    chip = x * YS + t // CORES
    place = x * TS + t

    def plane_id(other):
        return {"dp": other // TS, "tm": other % TS}

    def chip_id(other):
        return {"dp": other // YS, "tm": (other % YS) * CORES + core}

    barrier = pltpu.get_barrier_semaphore()

    @pl.loop(1, PLANE)
    def _(step):
        pl.semaphore_signal(barrier, inc=1, device_id=plane_id((place + step) % PLANE))

    @pl.loop(1, ZS)
    def _(step):
        pl.semaphore_signal(barrier, inc=1, device_id={"rows": (z + step) % ZS})

    loads = [
        pltpu.make_async_copy(clips, xh.at[0, :, pl.ds(1, ROWS)], load.at[0]),
        pltpu.make_async_copy(space_w.at[0], ws.at[0], load.at[1]),
        pltpu.make_async_copy(time_w, wt, load.at[2]),
        pltpu.make_async_copy(upstream, grads.at[1, pl.ds(0, OWN)], load.at[3]),
        pltpu.make_async_copy(space_w.at[1], ws.at[1], load.at[4]),
    ]
    for copy in loads:
        copy.start()

    blank_row = jnp.zeros((OWN, COLS, C), BF)
    blank = jnp.zeros((OWN, ROWS, COLS, C), BF)

    @pl.when(z == 0)
    def _():
        for layer in range(2):
            xh[layer, :, 0] = blank_row
            dh[layer, :, 0] = blank_row

    @pl.when(z == ZS - 1)
    def _():
        for layer in range(2):
            xh[layer, :, ROWS + 1] = blank_row
            dh[layer, :, ROWS + 1] = blank_row

    @pl.when(t == 0)
    def _():
        for layer in range(2):
            acts[layer, :OWN] = blank

    @pl.when(t == TS - 1)
    def _():
        for layer in range(2):
            grads[layer, OWN:] = blank

    def halo(number, low, high, buffer):
        up = pltpu.make_async_remote_copy(
            src_ref=high, dst_ref=buffer.at[:, 0], send_sem=halo_s.at[number, 0], recv_sem=halo_r.at[number, 0],
            device_id={"rows": jnp.minimum(z + 1, ZS - 1)},
        )
        down = pltpu.make_async_remote_copy(
            src_ref=low, dst_ref=buffer.at[:, ROWS + 1], send_sem=halo_s.at[number, 1], recv_sem=halo_r.at[number, 1],
            device_id={"rows": jnp.maximum(z - 1, 0)},
        )
        return up, down

    def halo_start(pair):
        pl.when(z < ZS - 1)(pair[0].start)
        pl.when(z > 0)(pair[1].start)

    def halo_arrived(pair):
        pl.when(z > 0)(pair[0].wait_recv)
        pl.when(z < ZS - 1)(pair[1].wait_recv)

    def halo_sent(pair):
        pl.when(z < ZS - 1)(pair[0].wait_send)
        pl.when(z > 0)(pair[1].wait_send)

    def later(number, source, target):
        return pltpu.make_async_remote_copy(
            src_ref=source, dst_ref=target, send_sem=time_s.at[number], recv_sem=time_r.at[number],
            device_id={"tm": jnp.minimum(t + 1, TS - 1)},
        )

    def earlier(number, source, target):
        return pltpu.make_async_remote_copy(
            src_ref=source, dst_ref=target, send_sem=time_s.at[number], recv_sem=time_r.at[number],
            device_id={"tm": jnp.maximum(t - 1, 0)},
        )

    x_halo = [
        halo(0, clips.at[:, 0], clips.at[:, ROWS - 1], xh.at[0]),
        halo(1, xh.at[1, :, 1], xh.at[1, :, ROWS], xh.at[1]),
    ]
    d_halo = [
        halo(2, dh.at[0, :, 1], dh.at[0, :, ROWS], dh.at[0]),
        halo(3, dh.at[1, :, 1], dh.at[1, :, ROWS], dh.at[1]),
    ]
    act_copy = [later(layer, acts.at[layer, pl.ds(OWN, OWN)], acts.at[layer, pl.ds(0, OWN)]) for layer in range(2)]
    grad_copy = [
        earlier(2, grads.at[0, pl.ds(0, OWN)], grads.at[0, pl.ds(OWN, OWN)]),
        earlier(3, upstream, grads.at[1, pl.ds(OWN, OWN)]),
    ]

    def one_clip(frame, offset):
        first = jnp.maximum(frame - offset, 0)
        same = (frame - offset >= 0) & (frame < FRAMES) & (seg[0, first] == seg[0, jnp.minimum(frame, FRAMES - 1)])
        return jnp.where(same, 1.0, 0.0)

    first_frame = t * OWN
    back_mask = [[one_clip(first_frame + i, k) for i in range(OWN)] for k in range(3)]
    next_mask = [[one_clip(first_frame + i + k, k) for i in range(OWN)] for k in range(3)]

    def gated(values, mask):
        return (values.astype(F32) * mask).astype(BF)

    def temporal(layer):
        columns = []
        for k in range(3):
            frames = [acts[layer, OWN + i - k] for i in range(OWN)]
            if k:
                frames = [gated(frames[i], back_mask[k][i]) for i in range(OWN)]
            columns.append(jnp.stack(frames).reshape(CELLS, C))
        out = mm(jnp.concatenate(columns, axis=1), wt[layer].reshape(3 * C, C))
        return (xh[layer, :, 1 : ROWS + 1].astype(F32) + out.reshape(OWN, ROWS, COLS, C)).astype(BF)

    def lifted(layer, k):
        frames = [grads[layer, i + k] for i in range(OWN)]
        if k:
            frames = [gated(frames[i], next_mask[k][i]) for i in range(OWN)]
        return jnp.stack(frames).reshape(CELLS, C)

    def activate(layer):
        pre = spatial(xh.at[layer], ws.at[layer])
        sigma = jax.nn.sigmoid(pre)
        acts[layer, OWN:] = (pre * sigma).astype(BF).reshape(OWN, ROWS, COLS, C)
        slopes[layer] = sigma * (1.0 + pre * (1.0 - sigma))

    def grad_of_act(layer):
        out = mm_nt(lifted(layer, 0), wt[layer, 0])
        for k in range(1, 3):
            out = out + mm_nt(lifted(layer, k), wt[layer, k])
        return out

    pl.semaphore_wait(barrier, PLANE - 1 + ZS - 1)
    halo_start(x_halo[0])
    pl.when(t > 0)(grad_copy[1].start)

    loads[0].wait()
    loads[1].wait()
    halo_arrived(x_halo[0])
    activate(0)
    pl.when(t < TS - 1)(act_copy[0].start)
    for i in range(OWN):
        turned[:, (OWN + i) * 256 : (OWN + i + 1) * 256] = acts[0, OWN + i].reshape(256, C).T
    loads[2].wait()
    loads[3].wait()
    loads[4].wait()
    pl.when(t < TS - 1)(grad_copy[1].wait_recv)
    dact[...] = grad_of_act(1)

    pl.when(t > 0)(act_copy[0].wait_recv)
    xh[1, :, 1 : ROWS + 1] = temporal(0)
    halo_start(x_halo[1])
    for i in range(OWN):
        turned[:, i * 256 : (i + 1) * 256] = acts[0, i].reshape(256, C).T
    halo_arrived(x_halo[1])

    activate(1)
    dh[1, :, 1 : ROWS + 1] = (dact[...] * slopes[1]).astype(BF).reshape(OWN, ROWS, COLS, C)
    halo_start(d_halo[1])
    pl.when(t < TS - 1)(act_copy[1].start)
    own_turned = acts[1, OWN:].reshape(CELLS, C).T
    for k in range(3):
        part[(3 + k) * C : (4 + k) * C] = mm(own_turned, lifted(1, k))
    halo_arrived(d_halo[1])

    back = spatial_back(dh.at[1], ws.at[1])
    first_grad = grads[1, :OWN].reshape(CELLS, C).astype(F32) + back
    grads[0, :OWN] = first_grad.astype(BF).reshape(OWN, ROWS, COLS, C)
    pl.when(t > 0)(grad_copy[0].start)
    for k in range(3):
        frames = [grads[0, i] for i in range(OWN)]
        if k:
            frames = [gated(frames[i], back_mask[k][i]) for i in range(OWN)]
        part[k * C : (k + 1) * C] = mm(
            turned[:, (OWN - k) * 256 : (2 * OWN - k) * 256], jnp.stack(frames).reshape(CELLS, C)
        )

    @pl.loop(0, XS)
    def _(high):
        for block in range(ZS):
            rows = part[pl.ds(pl.multiple_of(96 * block + PIECE * YS * high, 8), PIECE * YS), :]
            for low in range(YS):
                arranged[high * YS + low, PIECE * block : PIECE * (block + 1), :] = rows[
                    PIECE * low : PIECE * (low + 1)
                ]

    @pl.loop(0, CHIPS)
    def _(group):
        rows = arranged[group]
        other = jnp.where(core == 0, rows[:, HALF:], rows[:, :HALF])
        send_pair[group] = other.astype(BF)

    pair = pltpu.make_async_remote_copy(
        src_ref=send_pair, dst_ref=recv_pair, send_sem=sums.at[0], recv_sem=sums.at[1],
        device_id={"tm": t + 1 - 2 * core},
    )
    pair.start()
    pair.wait()

    @pl.loop(0, CHIPS)
    def _(group):
        rows = arranged[group]
        own = jnp.where(core == 0, rows[:, :HALF], rows[:, HALF:])
        send_plane[group] = (own + recv_pair[group].astype(F32)).astype(BF)

    @pl.loop(1, CHIPS)
    def _(step):
        other = (chip + step) % CHIPS
        pltpu.make_async_remote_copy(
            src_ref=send_plane.at[other], dst_ref=recv_plane.at[chip], send_sem=sums.at[2], recv_sem=sums.at[3],
            device_id=chip_id(other),
        ).start()

    recv_plane[chip] = send_plane[chip]

    pl.when(t < TS - 1)(grad_copy[0].wait_recv)
    dh[0, :, 1 : ROWS + 1] = (grad_of_act(0) * slopes[0]).astype(BF).reshape(OWN, ROWS, COLS, C)
    halo_start(d_halo[0])

    pltpu.make_async_remote_copy(
        src_ref=send_plane.at[pl.ds(0, CHIPS - 1)], dst_ref=recv_plane.at[pl.ds(0, CHIPS - 1)],
        send_sem=sums.at[2], recv_sem=sums.at[3], device_id=chip_id((chip + 1) % CHIPS),
    ).wait()
    summed = recv_plane[0].astype(F32)
    for group in range(1, CHIPS):
        summed = summed + recv_plane[group].astype(F32)
    for block in range(ZS):
        send_z[block, :PIECE, :] = summed[PIECE * block : PIECE * (block + 1), :]
        send_z[block, PIECE:, :] = jnp.zeros((8 - PIECE, HALF), F32)

    @pl.loop(1, ZS)
    def _(step):
        other = (z + step) % ZS
        pltpu.make_async_remote_copy(
            src_ref=send_z.at[other], dst_ref=recv_z.at[z], send_sem=sums.at[4], recv_sem=sums.at[5],
            device_id={"rows": other},
        ).start()

    recv_z[z] = send_z[z]

    pl.when(t > 0)(act_copy[1].wait_recv)
    feat[...] = temporal(1)
    feat_store = pltpu.make_async_copy(feat, feat_out, store.at[0])
    feat_store.start()
    halo_arrived(d_halo[0])
    gin[...] = (grads[0, :OWN].reshape(CELLS, C).astype(F32) + spatial_back(dh.at[0], ws.at[0])).astype(BF).reshape(
        OWN, ROWS, COLS, C
    )
    gin_store = pltpu.make_async_copy(gin, grad_out, store.at[1])
    gin_store.start()

    pltpu.make_async_remote_copy(
        src_ref=send_z.at[pl.ds(0, ZS - 1)], dst_ref=recv_z.at[pl.ds(0, ZS - 1)],
        send_sem=sums.at[4], recv_sem=sums.at[5], device_id={"rows": (z + 1) % ZS},
    ).wait()
    final = recv_z[0]
    for block in range(1, ZS):
        final = final + recv_z[block]
    total[...] = final

    @pl.loop(1, PLANE)
    def _(step):
        pltpu.make_async_remote_copy(
            src_ref=total, dst_ref=recv_all.at[place], send_sem=sums.at[6], recv_sem=sums.at[7],
            device_id=plane_id((place + step) % PLANE),
        ).start()

    recv_all[place] = final
    for pair in x_halo + d_halo:
        halo_sent(pair)
    for copy in act_copy:
        pl.when(t < TS - 1)(copy.wait_send)
    for copy in grad_copy:
        pl.when(t > 0)(copy.wait_send)
    feat_store.wait()
    gin_store.wait()
    pltpu.make_async_remote_copy(
        src_ref=recv_all.at[pl.ds(0, PLANE - 1)], dst_ref=recv_all.at[pl.ds(0, PLANE - 1)],
        send_sem=sums.at[6], recv_sem=sums.at[7], device_id=plane_id((place + 1) % PLANE),
    ).wait()
    for group in range(CHIPS):
        for half in range(CORES):
            result[PIECE * group : PIECE * (group + 1), HALF * half : HALF * (half + 1)] = recv_all[
                group * CORES + half, :PIECE, :
            ]
    weight_store = pltpu.make_async_copy(result, weight_out, store.at[2])
    weight_store.start()
    weight_store.wait()


def local(clips, segment_ids, spatial_weight, temporal_weight, upstream):
    deep = PIECE * ZS
    cells = (OWN, ROWS, COLS, C)
    anywhere = pl.BlockSpec(memory_space=pl.ANY)
    grad, features, weight_grad = pl.pallas_call(
        kernel,
        out_shape=(
            jax.ShapeDtypeStruct(cells, BF),
            jax.ShapeDtypeStruct(cells, BF),
            jax.ShapeDtypeStruct((6 * C // ZS, C), F32),
        ),
        in_specs=[pl.BlockSpec(memory_space=pltpu.SMEM)] + [anywhere] * 4,
        out_specs=(anywhere,) * 3,
        scratch_shapes=[
            pltpu.VMEM((2, 3, 3, C, C), BF),
            pltpu.VMEM((2, 3, C, C), BF),
            pltpu.VMEM((2, OWN, ROWS + 2, COLS, C), BF),
            pltpu.VMEM((2, 2 * OWN, ROWS, COLS, C), BF),
            pltpu.VMEM((2, CELLS, C), F32),
            pltpu.VMEM((2, 2 * OWN, ROWS, COLS, C), BF),
            pltpu.VMEM((2, OWN, ROWS + 2, COLS, C), BF),
            pltpu.VMEM((CELLS, C), F32),
            pltpu.VMEM((C, 2 * CELLS), BF),
            pltpu.VMEM((6 * C, C), F32),
            pltpu.VMEM(cells, BF),
            pltpu.VMEM(cells, BF),
            pltpu.VMEM((CHIPS, deep, C), F32),
            pltpu.VMEM((CHIPS, deep, HALF), BF),
            pltpu.VMEM((CHIPS, deep, HALF), BF),
            pltpu.VMEM((CHIPS, deep, HALF), BF),
            pltpu.VMEM((CHIPS, deep, HALF), BF),
            pltpu.VMEM((ZS, 8, HALF), F32),
            pltpu.VMEM((ZS, 8, HALF), F32),
            pltpu.VMEM((8, HALF), F32),
            pltpu.VMEM((PLANE, 8, HALF), F32),
            pltpu.VMEM((6 * C // ZS, C), F32),
            pltpu.SemaphoreType.DMA((5,)),
            pltpu.SemaphoreType.DMA((4, 2)),
            pltpu.SemaphoreType.DMA((4, 2)),
            pltpu.SemaphoreType.DMA((4,)),
            pltpu.SemaphoreType.DMA((4,)),
            pltpu.SemaphoreType.DMA((8,)),
            pltpu.SemaphoreType.DMA((3,)),
        ],
        compiler_params=pltpu.CompilerParams(
            collective_id=0, has_side_effects=True, vmem_limit_bytes=56 * 1024 * 1024
        ),
    )(
        segment_ids,
        clips.reshape(cells),
        spatial_weight.reshape(2, 3, 3, C, C),
        temporal_weight,
        upstream.reshape(cells),
    )
    return (grad.reshape(clips.shape), features.reshape(clips.shape), weight_grad)


def solution(mesh):
    return jax.shard_map(
        local,
        mesh=mesh,
        in_specs=(
            P("dp", "tm", "rows", None, None),
            P("dp", None),
            P(),
            P(),
            P("dp", "tm", "rows", None, None),
        ),
        out_specs=(
            P("dp", "tm", "rows", None, None),
            P("dp", "tm", "rows", None, None),
            P("rows", None),
        ),
        check_vma=False,
    )
```

```python
import jax
import jax.numpy as jnp
from jax import lax
from jax.experimental import pallas as pl
from jax.experimental.pallas import tpu as pltpu
from jax.sharding import PartitionSpec as P

XS, YS, CORES, ZS = 4, 4, 2, 16
TS = YS * CORES
CHIPS = XS * YS
PLANE = CHIPS * CORES
PIECE = 6
HALF = 128
C = 256
COLS = 64
ROWS = 4
OWN = 2
CELLS = OWN * ROWS * COLS
FRAMES = TS * OWN
DEEP = ZS // 2
BF, F32 = jnp.bfloat16, jnp.float32
NT = (((1,), (1,)), ((), ()))


def mm(left, right):
    return jnp.dot(left, right, preferred_element_type=F32)


def mm_nt(left, right):
    return lax.dot_general(left, right, NT, preferred_element_type=F32)


def rows_of(padded, first, rows):
    return padded[:, first : first + rows].reshape(OWN * rows * COLS, C)


def shifted(values, by):
    column = lax.broadcasted_iota(jnp.int32, values.shape, 0) % COLS
    edge = 0 if by == 1 else COLS - 1
    return jnp.where(column == edge, 0.0, pltpu.roll(values, by % values.shape[0], 0))


def spatial(padded, weights, rows):
    sums = []
    for kx in range(3):
        left = jnp.concatenate([rows_of(padded, ky, rows) for ky in range(3)], axis=1)
        right = jnp.concatenate([weights[ky, kx] for ky in range(3)], axis=0)
        sums.append(mm(left, right))
    return shifted(sums[0], 1) + sums[1] + shifted(sums[2], -1)


def spatial_back(padded, weights):
    sums = []
    for kx in range(3):
        total = None
        for ky in range(3):
            part = mm_nt(rows_of(padded, 2 - ky, ROWS), weights[ky, kx])
            total = part if total is None else total + part
        sums.append(total)
    return shifted(sums[0], -1) + sums[1] + shifted(sums[2], 1)


def finish(grad_in, feat_in, weight_in, grad_out, feat_out, weight_out, done):
    pairs = ((grad_in, grad_out), (feat_in, feat_out), (weight_in, weight_out))
    copies = [pltpu.make_async_copy(pair[0], pair[1], done.at[i]) for i, pair in enumerate(pairs)]
    for copy in copies:
        copy.start()
    for copy in copies:
        copy.wait()


def kernel(
    seg, clips, space_w, time_w, upstream,
    grad_out, feat_out, weight_out,
    ws, wt, x0, x1, act0, act1, slope0, slope1, g2, g1, dpre1, dpre0, dact, turned, part, feat, gin,
    arranged, send_pair, recv_pair, send_plane, recv_plane, send_z, recv_z, total, recv_all, result,
    load, wide_s, wide_r, near_s, near_r, sums, store, known,
):
    x = lax.axis_index("dp")
    t = lax.axis_index("tm")
    z = lax.axis_index("rows")
    core = t % CORES
    chip = x * YS + t // CORES
    place = x * TS + t

    def at(dx, dt, dz):
        return {"dp": (x + dx) % XS, "tm": (t + dt) % TS, "rows": (z + dz) % ZS}

    def plane_id(other):
        return {"dp": other // TS, "tm": other % TS}

    def chip_id(other):
        return {"dp": other // YS, "tm": (other % YS) * CORES + core}

    near = [(0, dt, dz) for dt in (-1, 0, 1) for dz in (-1, 0, 1) if dt or dz]
    near += [(-1, 0, 0), (1, 0, 0), (0, -2, 0), (0, 2, 0)]
    second = [(0, 0, -2), (0, 0, 2), (-1, 0, 0), (1, 0, 0), (2, 0, 0)]
    third = [(0, 0, -4), (0, 0, 4)]

    def tell(semaphore, partners):
        for partner in partners:
            pl.semaphore_signal(semaphore, inc=1, device_id=at(*partner))

    barrier = pltpu.get_barrier_semaphore()
    tell(barrier, near)

    loads = [
        pltpu.make_async_copy(clips, x0.at[pl.ds(OWN, OWN), pl.ds(3, ROWS)], load.at[0]),
        pltpu.make_async_copy(space_w.at[0], ws.at[0], load.at[1]),
        pltpu.make_async_copy(time_w, wt, load.at[2]),
        pltpu.make_async_copy(upstream, g2.at[pl.ds(0, OWN), pl.ds(1, ROWS)], load.at[3]),
        pltpu.make_async_copy(space_w.at[1], ws.at[1], load.at[4]),
    ]
    for copy in loads:
        copy.start()

    def blank(ref):
        ref[...] = jnp.zeros(ref.shape, ref.dtype)

    first, last = z == 0, z == ZS - 1
    early, late = t == 0, t == TS - 1

    @pl.when(first)
    def _():
        blank(x0.at[:, pl.ds(0, 3)])
        blank(g2.at[:, pl.ds(0, 1)])
        blank(dpre0.at[:, pl.ds(0, 1)])

    @pl.when(last)
    def _():
        blank(x0.at[:, pl.ds(ROWS + 3, 3)])
        blank(g2.at[:, pl.ds(ROWS + 1, 1)])
        blank(dpre0.at[:, pl.ds(ROWS + 1, 1)])

    @pl.when(early)
    def _():
        blank(x0.at[pl.ds(0, OWN)])
        blank(act1.at[pl.ds(0, OWN)])

    @pl.when(late)
    def _():
        blank(g2.at[pl.ds(OWN, OWN)])
        blank(g1.at[pl.ds(OWN, OWN)])

    def remote(source, target, sems_s, sems_r, number, dt, dz):
        copy = pltpu.make_async_remote_copy(
            src_ref=source, dst_ref=target, send_sem=sems_s.at[number], recv_sem=sems_r.at[number],
            device_id=at(0, dt, dz),
        )
        sends, takes = [], []
        if dt == 1:
            sends.append(t < TS - 1)
            takes.append(t > 0)
        if dt == -1:
            sends.append(t > 0)
            takes.append(t < TS - 1)
        if dz == 1:
            sends.append(z < ZS - 1)
            takes.append(z > 0)
        if dz == -1:
            sends.append(z > 0)
            takes.append(z < ZS - 1)
        send, take = sends[0], takes[0]
        for more in sends[1:]:
            send = send & more
        for more in takes[1:]:
            take = take & more
        return copy, send, take

    def start(group):
        for copy, send, _ in group:
            pl.when(send)(copy.start)

    def arrived(group):
        for copy, _, take in group:
            pl.when(take)(copy.wait_recv)

    def sent(group):
        for copy, send, _ in group:
            pl.when(send)(copy.wait_send)

    x_low, x_high = clips.at[:, pl.ds(0, 3)], clips.at[:, pl.ds(1, 3)]
    prior, own = pl.ds(0, OWN), pl.ds(OWN, OWN)
    top, middle, bottom = pl.ds(0, 3), pl.ds(3, ROWS), pl.ds(ROWS + 3, 3)
    x_halo = [
        remote(x_high, x0.at[own, top], wide_s, wide_r, 0, 0, 1),
        remote(x_low, x0.at[own, bottom], wide_s, wide_r, 1, 0, -1),
    ]
    x_prior = [remote(clips, x0.at[prior, middle], wide_s, wide_r, 2, 1, 0)]
    x_corner = [
        remote(x_high, x0.at[prior, top], wide_s, wide_r, 3, 1, 1),
        remote(x_low, x0.at[prior, bottom], wide_s, wide_r, 4, 1, -1),
    ]
    g_low, g_high = upstream.at[:, pl.ds(0, 1)], upstream.at[:, pl.ds(ROWS - 1, 1)]
    now, after = pl.ds(0, OWN), pl.ds(OWN, OWN)
    over, inner, under = pl.ds(0, 1), pl.ds(1, ROWS), pl.ds(ROWS + 1, 1)
    g_halo = [
        remote(g_high, g2.at[now, over], wide_s, wide_r, 5, 0, 1),
        remote(g_low, g2.at[now, under], wide_s, wide_r, 6, 0, -1),
        remote(upstream, g2.at[after, inner], wide_s, wide_r, 7, -1, 0),
        remote(g_high, g2.at[after, over], wide_s, wide_r, 8, -1, 1),
        remote(g_low, g2.at[after, under], wide_s, wide_r, 9, -1, -1),
    ]
    act_copy = [remote(act1.at[own], act1.at[prior], near_s, near_r, 0, 1, 0)]
    g1_copy = [remote(g1.at[now], g1.at[after], near_s, near_r, 1, -1, 0)]
    d_halo = [
        remote(dpre0.at[:, pl.ds(ROWS, 1)], dpre0.at[:, over], near_s, near_r, 2, 0, 1),
        remote(dpre0.at[:, pl.ds(1, 1)], dpre0.at[:, under], near_s, near_r, 3, 0, -1),
    ]

    def one_clip(frame, offset):
        before = jnp.maximum(frame - offset, 0)
        same = (frame - offset >= 0) & (frame < FRAMES) & (seg[0, before] == seg[0, jnp.minimum(frame, FRAMES - 1)])
        return jnp.where(same, 1.0, 0.0)

    first_frame = t * OWN
    back_mask = [[one_clip(first_frame + i, k) for i in range(OWN)] for k in range(3)]
    next_mask = [[one_clip(first_frame + i + k, k) for i in range(OWN)] for k in range(3)]

    def gated(values, mask):
        return (values.astype(F32) * mask).astype(BF)

    def temporal(base, acts, weights):
        rows = base.shape[1]
        columns = []
        for k in range(3):
            frames = [acts[OWN + i - k] for i in range(OWN)]
            if k:
                frames = [gated(frames[i], back_mask[k][i]) for i in range(OWN)]
            columns.append(jnp.stack(frames).reshape(OWN * rows * COLS, C))
        out = mm(jnp.concatenate(columns, axis=1), weights.reshape(3 * C, C))
        return (base.astype(F32) + out.reshape(base.shape)).astype(BF)

    def lifted(grads, k):
        frames = [grads[i + k] for i in range(OWN)]
        if k:
            frames = [gated(frames[i], next_mask[k][i]) for i in range(OWN)]
        return jnp.stack(frames).reshape(OWN * frames[0].shape[0] * COLS, C)

    def grad_of_act(grads, weights):
        out = mm_nt(lifted(grads, 0), weights[0])
        for k in range(1, 3):
            out = out + mm_nt(lifted(grads, k), weights[k])
        return out

    def slope(pre, sigma):
        return sigma * (1.0 + pre * (1.0 - sigma))

    pl.semaphore_wait(barrier, len(near))
    start(x_halo)
    start(x_prior)
    start(x_corner)
    tell(known.at[0], near)

    loads[0].wait()
    loads[1].wait()
    arrived(x_halo)
    start(g_halo)
    wide = (OWN, ROWS + 4, COLS, C)
    pre = spatial(x0.at[own], ws.at[0], ROWS + 4)
    sigma = jax.nn.sigmoid(pre)
    act0[OWN:] = (pre * sigma).astype(BF).reshape(wide)
    slope0[...] = slope(pre, sigma).reshape(wide)[:, 2 : ROWS + 2].reshape(CELLS, C)
    pl.semaphore_wait(known.at[0], len(near))
    tell(known.at[1], second)

    def turn(i):
        turned[:, i * 256 : (i + 1) * 256] = act0[i, 2 : ROWS + 2].reshape(256, C).T

    for i in range(OWN):
        turn(OWN + i)
    loads[2].wait()
    loads[3].wait()
    loads[4].wait()
    arrived(x_prior)
    arrived(x_corner)
    pre = spatial(x0.at[prior], ws.at[0], ROWS + 4)
    act0[:OWN] = (pre * jax.nn.sigmoid(pre)).astype(BF).reshape(wide)
    x1[...] = temporal(x0[OWN:, 1 : ROWS + 5], act0, wt[0])

    @pl.when(first)
    def _():
        blank(x1.at[:, pl.ds(0, 2)])

    @pl.when(last)
    def _():
        blank(x1.at[:, pl.ds(ROWS + 2, 2)])

    tall = (OWN, ROWS + 2, COLS, C)
    pre = spatial(x1, ws.at[1], ROWS + 2)
    sigma = jax.nn.sigmoid(pre)
    act1[OWN:] = (pre * sigma).astype(BF).reshape(tall)[:, 1 : ROWS + 1]
    slope1[...] = slope(pre, sigma)
    start(act_copy)
    arrived(g_halo)
    dact[...] = grad_of_act(g2, wt[1])
    dpre1[...] = (dact[...] * slope1[...]).astype(BF).reshape(tall)

    @pl.when(first)
    def _():
        blank(dpre1.at[:, over])

    @pl.when(last)
    def _():
        blank(dpre1.at[:, under])

    g1[:OWN] = (
        g2[:OWN, 1 : ROWS + 1].astype(F32) + spatial_back(dpre1, ws.at[1]).reshape(OWN, ROWS, COLS, C)
    ).astype(BF)
    start(g1_copy)
    for i in range(OWN):
        turn(i)
    for k in range(3):
        frames = [g1[i] for i in range(OWN)]
        if k:
            frames = [gated(frames[i], back_mask[k][i]) for i in range(OWN)]
        part[0, k * C : (k + 1) * C] = mm(
            turned[:, (OWN - k) * 256 : (2 * OWN - k) * 256], jnp.stack(frames).reshape(CELLS, C)
        )

    def pair_copy(layer):
        return pltpu.make_async_remote_copy(
            src_ref=send_pair.at[layer], dst_ref=recv_pair.at[layer], send_sem=sums.at[layer],
            recv_sem=sums.at[2 + layer], device_id={"tm": t + 1 - 2 * core},
        )

    def arrange(layer):
        @pl.loop(0, XS)
        def _(high):
            for block in range(DEEP):
                rows = part[layer, pl.ds(pl.multiple_of(96 * block + PIECE * YS * high, 8), PIECE * YS), :]
                for low in range(YS):
                    arranged[layer, high * YS + low, PIECE * block : PIECE * (block + 1), :] = rows[
                        PIECE * low : PIECE * (low + 1)
                    ]

        @pl.loop(0, CHIPS)
        def _(group):
            rows = arranged[layer, group]
            send_pair[layer, group] = jnp.where(core == 0, rows[:, HALF:], rows[:, :HALF]).astype(BF)

        pair_copy(layer).start()

    def spread(layer):
        pair_copy(layer).wait()

        @pl.loop(0, CHIPS)
        def _(group):
            rows = arranged[layer, group]
            mine = jnp.where(core == 0, rows[:, :HALF], rows[:, HALF:])
            send_plane[layer, group] = (mine + recv_pair[layer, group].astype(F32)).astype(BF)

        @pl.loop(1, CHIPS)
        def _(step):
            other = (chip + step) % CHIPS
            pltpu.make_async_remote_copy(
                src_ref=send_plane.at[layer, other], dst_ref=recv_plane.at[layer, chip],
                send_sem=sums.at[4 + layer], recv_sem=sums.at[6 + layer], device_id=chip_id(other),
            ).start()

        recv_plane[layer, chip] = send_plane[layer, chip]

    def gather(layer):
        pltpu.make_async_remote_copy(
            src_ref=send_plane.at[layer, pl.ds(0, CHIPS - 1)], dst_ref=recv_plane.at[layer, pl.ds(0, CHIPS - 1)],
            send_sem=sums.at[4 + layer], recv_sem=sums.at[6 + layer], device_id=chip_id((chip + 1) % CHIPS),
        ).wait()
        summed = recv_plane[layer, 0].astype(F32)
        for group in range(1, CHIPS):
            summed = summed + recv_plane[layer, group].astype(F32)
        for block in range(DEEP):
            send_z[layer * DEEP + block, :PIECE, :] = summed[PIECE * block : PIECE * (block + 1), :]
            send_z[layer * DEEP + block, PIECE:, :] = jnp.zeros((8 - PIECE, HALF), F32)

        @pl.loop(0, DEEP)
        def _(step):
            other = layer * DEEP + (z + step) % DEEP

            @pl.when(other != z)
            def _():
                pltpu.make_async_remote_copy(
                    src_ref=send_z.at[other], dst_ref=recv_z.at[z], send_sem=sums.at[8], recv_sem=sums.at[9],
                    device_id={"rows": other},
                ).start()

    arrange(0)
    turned_own = act1[OWN:].reshape(CELLS, C).T
    for k in range(3):
        frames = [g2[i + k, 1 : ROWS + 1] for i in range(OWN)]
        if k:
            frames = [gated(frames[i], next_mask[k][i]) for i in range(OWN)]
        part[1, k * C : (k + 1) * C] = mm(turned_own, jnp.stack(frames).reshape(CELLS, C))
    arrange(1)
    pl.semaphore_wait(known.at[1], len(second))
    tell(known.at[2], third)
    spread(0)
    spread(1)

    arrived(g1_copy)
    dpre0[:, 1 : ROWS + 1] = (grad_of_act(g1, wt[0]) * slope0[...]).astype(BF).reshape(OWN, ROWS, COLS, C)
    start(d_halo)
    pl.semaphore_wait(known.at[2], len(third))
    gather(0)
    gather(1)
    recv_z[z] = send_z[z]

    arrived(act_copy)
    feat[...] = temporal(x1[:, 2 : ROWS + 2], act1, wt[1])
    feat_store = pltpu.make_async_copy(feat, feat_out, store.at[0])
    feat_store.start()
    arrived(d_halo)
    gin[...] = (
        g1[:OWN].astype(F32) + spatial_back(dpre0, ws.at[0]).reshape(OWN, ROWS, COLS, C)
    ).astype(BF)
    gin_store = pltpu.make_async_copy(gin, grad_out, store.at[1])
    gin_store.start()

    pltpu.make_async_remote_copy(
        src_ref=send_z.at[pl.ds(0, ZS - 1)], dst_ref=recv_z.at[pl.ds(0, ZS - 1)],
        send_sem=sums.at[8], recv_sem=sums.at[9], device_id={"rows": (z + 1) % ZS},
    ).wait()
    final = recv_z[0]
    for block in range(1, ZS):
        final = final + recv_z[block]
    total[...] = final

    @pl.loop(1, PLANE)
    def _(step):
        pltpu.make_async_remote_copy(
            src_ref=total, dst_ref=recv_all.at[place], send_sem=sums.at[10], recv_sem=sums.at[11],
            device_id=plane_id((place + step) % PLANE),
        ).start()

    recv_all[place] = final
    for group in (x_halo, x_prior, x_corner, g_halo, act_copy, g1_copy, d_halo):
        sent(group)
    feat_store.wait()
    gin_store.wait()
    pltpu.make_async_remote_copy(
        src_ref=recv_all.at[pl.ds(0, PLANE - 1)], dst_ref=recv_all.at[pl.ds(0, PLANE - 1)],
        send_sem=sums.at[10], recv_sem=sums.at[11], device_id=plane_id((place + 1) % PLANE),
    ).wait()
    for group in range(CHIPS):
        for half in range(CORES):
            result[PIECE * group : PIECE * (group + 1), HALF * half : HALF * (half + 1)] = recv_all[
                group * CORES + half, :PIECE, :
            ]
    weight_store = pltpu.make_async_copy(result, weight_out, store.at[2])
    weight_store.start()
    weight_store.wait()


def local(clips, segment_ids, spatial_weight, temporal_weight, upstream):
    deep = PIECE * DEEP
    cells = (OWN, ROWS, COLS, C)
    anywhere = pl.BlockSpec(memory_space=pl.ANY)
    outs = (
        jax.ShapeDtypeStruct(cells, BF),
        jax.ShapeDtypeStruct(cells, BF),
        jax.ShapeDtypeStruct((6 * C // ZS, C), F32),
    )
    parts = pl.pallas_call(
        kernel,
        out_shape=outs,
        in_specs=[pl.BlockSpec(memory_space=pltpu.SMEM)] + [anywhere] * 4,
        out_specs=(anywhere,) * 3,
        scratch_shapes=[
            pltpu.VMEM((2, 3, 3, C, C), BF),
            pltpu.VMEM((2, 3, C, C), BF),
            pltpu.VMEM((2 * OWN, ROWS + 6, COLS, C), BF),
            pltpu.VMEM((OWN, ROWS + 4, COLS, C), BF),
            pltpu.VMEM((2 * OWN, ROWS + 4, COLS, C), BF),
            pltpu.VMEM((2 * OWN, ROWS, COLS, C), BF),
            pltpu.VMEM((CELLS, C), F32),
            pltpu.VMEM((OWN * (ROWS + 2) * COLS, C), F32),
            pltpu.VMEM((2 * OWN, ROWS + 2, COLS, C), BF),
            pltpu.VMEM((2 * OWN, ROWS, COLS, C), BF),
            pltpu.VMEM((OWN, ROWS + 2, COLS, C), BF),
            pltpu.VMEM((OWN, ROWS + 2, COLS, C), BF),
            pltpu.VMEM((OWN * (ROWS + 2) * COLS, C), F32),
            pltpu.VMEM((C, 2 * CELLS), BF),
            pltpu.VMEM((2, 3 * C, C), F32),
            pltpu.VMEM(cells, BF),
            pltpu.VMEM(cells, BF),
            pltpu.VMEM((2, CHIPS, deep, C), F32),
            pltpu.VMEM((2, CHIPS, deep, HALF), BF),
            pltpu.VMEM((2, CHIPS, deep, HALF), BF),
            pltpu.VMEM((2, CHIPS, deep, HALF), BF),
            pltpu.VMEM((2, CHIPS, deep, HALF), BF),
            pltpu.VMEM((ZS, 8, HALF), F32),
            pltpu.VMEM((ZS, 8, HALF), F32),
            pltpu.VMEM((8, HALF), F32),
            pltpu.VMEM((PLANE, 8, HALF), F32),
            pltpu.VMEM((6 * C // ZS, C), F32),
            pltpu.SemaphoreType.DMA((5,)),
            pltpu.SemaphoreType.DMA((10,)),
            pltpu.SemaphoreType.DMA((10,)),
            pltpu.SemaphoreType.DMA((4,)),
            pltpu.SemaphoreType.DMA((4,)),
            pltpu.SemaphoreType.DMA((12,)),
            pltpu.SemaphoreType.DMA((3,)),
            pltpu.SemaphoreType.REGULAR((3,)),
        ],
        compiler_params=pltpu.CompilerParams(
            collective_id=0, has_side_effects=True, vmem_limit_bytes=56 * 1024 * 1024
        ),
    )(
        segment_ids,
        clips.reshape(cells),
        spatial_weight.reshape(2, 3, 3, C, C),
        temporal_weight,
        upstream.reshape(cells),
    )
    grad, features, weight_grad = pl.pallas_call(
        finish,
        out_shape=outs,
        in_specs=[pl.BlockSpec(memory_space=pltpu.VMEM)] * 3,
        out_specs=(anywhere,) * 3,
        scratch_shapes=[pltpu.SemaphoreType.DMA((3,))],
    )(*parts)
    return (grad.reshape(clips.shape), features.reshape(clips.shape), weight_grad)


def solution(mesh):
    return jax.shard_map(
        local,
        mesh=mesh,
        in_specs=(
            P("dp", "tm", "rows", None, None),
            P("dp", None),
            P(),
            P(),
            P("dp", "tm", "rows", None, None),
        ),
        out_specs=(
            P("dp", "tm", "rows", None, None),
            P("dp", "tm", "rows", None, None),
            P("rows", None),
        ),
        check_vma=False,
    )
```

```python
import jax
import jax.numpy as jnp
from jax import lax
from jax.experimental import pallas as pl
from jax.experimental.pallas import tpu as pltpu
from jax.sharding import PartitionSpec as P

XS, YS, CORES, ZS = 4, 4, 2, 16
TS = YS * CORES
CHIPS = XS * YS
PLANE = CHIPS * CORES
PIECE = 6
HALF = 128
C = 256
COLS = 64
ROWS = 4
OWN = 2
CELLS = OWN * ROWS * COLS
FRAMES = TS * OWN
DEEP = ZS // 2
BF, F32 = jnp.bfloat16, jnp.float32


def mm(left, right):
    return jnp.dot(left, right, preferred_element_type=F32)


def rows_of(padded, first, rows):
    return padded[:, first : first + rows].reshape(OWN * rows * COLS, C)


def shifted(values, by):
    column = lax.broadcasted_iota(jnp.int32, values.shape, 0) % COLS
    edge = 0 if by == 1 else COLS - 1
    return jnp.where(column == edge, 0.0, pltpu.roll(values, by % values.shape[0], 0))


def spatial(padded, weights, rows):
    sums = []
    for kx in range(3):
        left = jnp.concatenate([rows_of(padded, ky, rows) for ky in range(3)], axis=1)
        right = jnp.concatenate([weights[ky, kx] for ky in range(3)], axis=0)
        sums.append(mm(left, right))
    return shifted(sums[0], 1) + sums[1] + shifted(sums[2], -1)


def spatial_back(padded, turned_weights):
    sums = []
    for kx in range(3):
        left = jnp.concatenate([rows_of(padded, 2 - ky, ROWS) for ky in range(3)], axis=1)
        right = jnp.concatenate([turned_weights[ky, kx] for ky in range(3)], axis=0)
        sums.append(mm(left, right))
    return shifted(sums[0], -1) + sums[1] + shifted(sums[2], 1)


def far_first(rows, columns):
    steps = [(i, j) for i in range(rows) for j in range(columns) if i or j]
    return sorted(steps, key=lambda step: -min(step[0], rows - step[0]) - min(step[1], columns - step[1]))


def finish(grad_in, feat_in, weight_in, grad_out, feat_out, weight_out, done):
    pairs = ((grad_in, grad_out), (feat_in, feat_out), (weight_in, weight_out))
    copies = [pltpu.make_async_copy(pair[0], pair[1], done.at[i]) for i, pair in enumerate(pairs)]
    for copy in copies:
        copy.start()
    for copy in copies:
        copy.wait()


def kernel(
    segments, clips, space_w, time_w, upstream,
    grad_out, feat_out, weight_out,
    ws, wt, wst, wtt, x0, x1, act0, act1, slope0, slope1, g2, g1, dpre1, dpre0, dact, turned, part,
    arranged, send_pair, recv_pair, send_plane, recv_plane, send_z, recv_z, total, recv_all,
    seg, load, wide_s, wide_r, near_s, near_r, sums, known,
):
    x = lax.axis_index("dp")
    t = lax.axis_index("tm")
    z = lax.axis_index("rows")
    core = t % CORES
    chip = x * YS + t // CORES
    place = x * TS + t

    def at(dx, dt, dz):
        return {"dp": (x + dx) % XS, "tm": (t + dt) % TS, "rows": (z + dz) % ZS}

    near = [(0, dt, dz) for dt in (-1, 0, 1) for dz in (-1, 0, 1) if dt or dz]
    near += [(-1, 0, 0), (1, 0, 0), (0, -2, 0), (0, 2, 0)]
    second = [(0, 0, -2), (0, 0, 2), (-1, 0, 0), (1, 0, 0), (2, 0, 0)]
    third = [(0, 0, -4), (0, 0, 4)]

    def tell(semaphore, partners):
        for partner in partners:
            pl.semaphore_signal(semaphore, inc=1, device_id=at(*partner))

    barrier = pltpu.get_barrier_semaphore()
    tell(barrier, near)

    loads = [
        pltpu.make_async_copy(clips, x0.at[pl.ds(OWN, OWN), pl.ds(3, ROWS)], load.at[0]),
        pltpu.make_async_copy(space_w.at[0], ws.at[0], load.at[1]),
        pltpu.make_async_copy(time_w, wt, load.at[2]),
        pltpu.make_async_copy(upstream, g2.at[pl.ds(0, OWN), pl.ds(1, ROWS)], load.at[3]),
        pltpu.make_async_copy(space_w.at[1], ws.at[1], load.at[4]),
        pltpu.make_async_copy(segments, seg, load.at[5]),
    ]
    for copy in loads:
        copy.start()

    def blank(ref):
        ref[...] = jnp.zeros(ref.shape, ref.dtype)

    first, last = z == 0, z == ZS - 1
    early, late = t == 0, t == TS - 1

    @pl.when(first)
    def _():
        blank(x0.at[:, pl.ds(0, 3)])
        blank(g2.at[:, pl.ds(0, 1)])
        blank(dpre0.at[:, pl.ds(0, 1)])

    @pl.when(last)
    def _():
        blank(x0.at[:, pl.ds(ROWS + 3, 3)])
        blank(g2.at[:, pl.ds(ROWS + 1, 1)])
        blank(dpre0.at[:, pl.ds(ROWS + 1, 1)])

    @pl.when(early)
    def _():
        blank(x0.at[pl.ds(0, OWN)])
        blank(act1.at[pl.ds(0, OWN)])

    @pl.when(late)
    def _():
        blank(g2.at[pl.ds(OWN, OWN)])
        blank(g1.at[pl.ds(OWN, OWN)])

    def remote(source, target, sems_s, sems_r, number, dt, dz, only=None, edge=0):
        copy = pltpu.make_async_remote_copy(
            src_ref=source, dst_ref=target, send_sem=sems_s.at[number], recv_sem=sems_r.at[number],
            device_id=at(0, dt, dz),
        )
        sends, takes = [], []
        if dt == 1:
            sends.append(t < TS - 1)
            takes.append(t > 0)
        if dt == -1:
            sends.append(t > 0)
            takes.append(t < TS - 1)
        if dz == 1:
            sends.append(z < ZS - 1)
            takes.append(z > 0)
        if dz == -1:
            sends.append(z > 0)
            takes.append(z < ZS - 1)
        if edge:
            inside = z > 0 if edge < 0 else z < ZS - 1
            sends.append(inside)
            takes.append(inside)
        if only is not None:
            sends.append(only)
            takes.append(jnp.logical_not(only))
        send, take = sends[0], takes[0]
        for more in sends[1:]:
            send = send & more
        for more in takes[1:]:
            take = take & more
        return copy, send, take

    def start(group):
        for copy, send, _ in group:
            pl.when(send)(copy.start)

    def arrived(group):
        for copy, _, take in group:
            pl.when(take)(copy.wait_recv)

    def sent(group):
        for copy, send, _ in group:
            pl.when(send)(copy.wait_send)

    x_low, x_high = clips.at[:, pl.ds(0, 3)], clips.at[:, pl.ds(1, 3)]
    prior, own = pl.ds(0, OWN), pl.ds(OWN, OWN)
    top, middle, bottom = pl.ds(0, 3), pl.ds(3, ROWS), pl.ds(ROWS + 3, 3)
    x_halo = [
        remote(x_high, x0.at[own, top], wide_s, wide_r, 0, 0, 1),
        remote(x_low, x0.at[own, bottom], wide_s, wide_r, 1, 0, -1),
    ]
    x_prior = [remote(clips, x0.at[prior, middle], wide_s, wide_r, 2, 1, 0)]
    x_corner = [
        remote(x_high, x0.at[prior, top], wide_s, wide_r, 3, 1, 1, core == 1),
        remote(x_low, x0.at[prior, bottom], wide_s, wide_r, 4, 1, -1, core == 1),
    ]
    x_handed = [
        remote(x0.at[own, top], x0.at[prior, top], wide_s, wide_r, 10, 1, 0, core == 0, -1),
        remote(x0.at[own, bottom], x0.at[prior, bottom], wide_s, wide_r, 11, 1, 0, core == 0, 1),
    ]
    g_low, g_high = upstream.at[:, pl.ds(0, 1)], upstream.at[:, pl.ds(ROWS - 1, 1)]
    now, after = pl.ds(0, OWN), pl.ds(OWN, OWN)
    over, inner, under = pl.ds(0, 1), pl.ds(1, ROWS), pl.ds(ROWS + 1, 1)
    g_halo = [
        remote(g_high, g2.at[now, over], wide_s, wide_r, 5, 0, 1),
        remote(g_low, g2.at[now, under], wide_s, wide_r, 6, 0, -1),
    ]
    g_later = [remote(upstream, g2.at[after, inner], wide_s, wide_r, 7, -1, 0)]
    g_corner = [
        remote(g_high, g2.at[after, over], wide_s, wide_r, 8, -1, 1, core == 0),
        remote(g_low, g2.at[after, under], wide_s, wide_r, 9, -1, -1, core == 0),
    ]
    g_handed = [
        remote(g2.at[now, over], g2.at[after, over], wide_s, wide_r, 12, -1, 0, core == 1, -1),
        remote(g2.at[now, under], g2.at[after, under], wide_s, wide_r, 13, -1, 0, core == 1, 1),
    ]
    act_copy = [remote(act1.at[own], act1.at[prior], near_s, near_r, 0, 1, 0)]
    g1_copy = [remote(g1.at[now], g1.at[after], near_s, near_r, 1, -1, 0)]
    d_halo = [
        remote(dpre0.at[:, pl.ds(ROWS, 1)], dpre0.at[:, over], near_s, near_r, 2, 0, 1),
        remote(dpre0.at[:, pl.ds(1, 1)], dpre0.at[:, under], near_s, near_r, 3, 0, -1),
    ]

    def gated(values, mask):
        return values * mask.astype(BF)

    def temporal(base, acts, weights):
        rows = base.shape[1]
        columns = []
        for k in range(3):
            frames = [acts[OWN + i - k] for i in range(OWN)]
            if k:
                frames = [gated(frames[i], back_mask[k][i]) for i in range(OWN)]
            columns.append(jnp.stack(frames).reshape(OWN * rows * COLS, C))
        out = mm(jnp.concatenate(columns, axis=1), weights.reshape(3 * C, C))
        return (base.astype(F32) + out.reshape(base.shape)).astype(BF)

    def lifted(grads, k):
        frames = [grads[i + k] for i in range(OWN)]
        if k:
            frames = [gated(frames[i], next_mask[k][i]) for i in range(OWN)]
        return jnp.stack(frames).reshape(OWN * frames[0].shape[0] * COLS, C)

    def grad_of_act(grads, turned_weights):
        left = jnp.concatenate([lifted(grads, k) for k in range(3)], axis=1)
        return mm(left, turned_weights.reshape(3 * C, C))

    def slope(pre, sigma):
        return sigma * (1.0 + pre * (1.0 - sigma))

    pl.semaphore_wait(barrier, len(near))
    start(x_halo)
    start(x_prior)
    start(x_corner)
    start(g_later)
    tell(known.at[0], near)

    for copy in loads:
        copy.wait()

    def one_clip(frame, offset):
        before = jnp.maximum(frame - offset, 0)
        same = (frame - offset >= 0) & (frame < FRAMES) & (seg[0, before] == seg[0, jnp.minimum(frame, FRAMES - 1)])
        return jnp.where(same, 1.0, 0.0)

    first_frame = t * OWN
    back_mask = [[one_clip(first_frame + i, k) for i in range(OWN)] for k in range(3)]
    next_mask = [[one_clip(first_frame + i + k, k) for i in range(OWN)] for k in range(3)]

    @pl.loop(0, 3)
    def _(index):
        for layer in range(2):
            for kx in range(3):
                wst[layer, index, kx] = ws[layer, index, kx].T
            wtt[layer, index] = wt[layer, index].T

    arrived(x_halo)
    start(x_handed)
    start(g_halo)
    start(g_corner)
    wide = (OWN, ROWS + 4, COLS, C)
    pre = spatial(x0.at[own], ws.at[0], ROWS + 4)
    sigma = jax.nn.sigmoid(pre)
    act0[OWN:] = (pre * sigma).astype(BF).reshape(wide)
    slope0[...] = slope(pre, sigma).reshape(wide)[:, 2 : ROWS + 2].reshape(CELLS, C)
    pl.semaphore_wait(known.at[0], len(near))
    tell(known.at[1], second)

    def turn(i):
        turned[:, i * 256 : (i + 1) * 256] = act0[i, 2 : ROWS + 2].reshape(256, C).T

    for i in range(OWN):
        turn(OWN + i)
    arrived(x_prior)
    arrived(x_corner)
    arrived(x_handed)
    pre = spatial(x0.at[prior], ws.at[0], ROWS + 4)
    act0[:OWN] = (pre * jax.nn.sigmoid(pre)).astype(BF).reshape(wide)
    arrived(g_halo)
    start(g_handed)
    x1[...] = temporal(x0[OWN:, 1 : ROWS + 5], act0, wt[0])

    @pl.when(first)
    def _():
        blank(x1.at[:, pl.ds(0, 2)])

    @pl.when(last)
    def _():
        blank(x1.at[:, pl.ds(ROWS + 2, 2)])

    tall = (OWN, ROWS + 2, COLS, C)
    pre = spatial(x1, ws.at[1], ROWS + 2)
    sigma = jax.nn.sigmoid(pre)
    act1[OWN:] = (pre * sigma).astype(BF).reshape(tall)[:, 1 : ROWS + 1]
    slope1[...] = slope(pre, sigma)
    start(act_copy)
    arrived(g_later)
    arrived(g_corner)
    arrived(g_handed)
    dact[...] = grad_of_act(g2, wtt[1])
    dpre1[...] = (dact[...] * slope1[...]).astype(BF).reshape(tall)

    @pl.when(first)
    def _():
        blank(dpre1.at[:, over])

    @pl.when(last)
    def _():
        blank(dpre1.at[:, under])

    g1[:OWN] = (
        g2[:OWN, 1 : ROWS + 1].astype(F32) + spatial_back(dpre1, wst.at[1]).reshape(OWN, ROWS, COLS, C)
    ).astype(BF)
    start(g1_copy)
    for i in range(OWN):
        turn(i)
    for k in range(3):
        frames = [g1[i] for i in range(OWN)]
        if k:
            frames = [gated(frames[i], back_mask[k][i]) for i in range(OWN)]
        part[0, k * C : (k + 1) * C] = mm(
            turned[:, (OWN - k) * 256 : (2 * OWN - k) * 256], jnp.stack(frames).reshape(CELLS, C)
        )

    def pair_copy(layer):
        return pltpu.make_async_remote_copy(
            src_ref=send_pair.at[layer], dst_ref=recv_pair.at[layer], send_sem=sums.at[layer],
            recv_sem=sums.at[2 + layer], device_id={"tm": t + 1 - 2 * core},
        )

    def arrange(layer):
        @pl.loop(0, XS)
        def _(high):
            for block in range(DEEP):
                rows = part[layer, pl.ds(pl.multiple_of(96 * block + PIECE * YS * high, 8), PIECE * YS), :]
                for low in range(YS):
                    arranged[layer, high * YS + low, PIECE * block : PIECE * (block + 1), :] = rows[
                        PIECE * low : PIECE * (low + 1)
                    ]

        @pl.loop(0, CHIPS)
        def _(group):
            rows = arranged[layer, group]
            send_pair[layer, group] = jnp.where(core == 0, rows[:, HALF:], rows[:, :HALF]).astype(BF)

        pair_copy(layer).start()

    def spread(layer):
        pair_copy(layer).wait()

        @pl.loop(0, CHIPS)
        def _(group):
            rows = arranged[layer, group]
            mine = jnp.where(core == 0, rows[:, :HALF], rows[:, HALF:])
            send_plane[layer, group] = (mine + recv_pair[layer, group].astype(F32)).astype(BF)

        for dx, dy in far_first(XS, YS):
            target = at(dx, CORES * dy, 0)
            other = target["dp"] * YS + target["tm"] // CORES
            pltpu.make_async_remote_copy(
                src_ref=send_plane.at[layer, other], dst_ref=recv_plane.at[layer, chip],
                send_sem=sums.at[4 + layer], recv_sem=sums.at[6 + layer], device_id=target,
            ).start()

        recv_plane[layer, chip] = send_plane[layer, chip]

    def gather(layer):
        pltpu.make_async_remote_copy(
            src_ref=send_plane.at[layer, pl.ds(0, CHIPS - 1)], dst_ref=recv_plane.at[layer, pl.ds(0, CHIPS - 1)],
            send_sem=sums.at[4 + layer], recv_sem=sums.at[6 + layer], device_id=at(1, 0, 0),
        ).wait()
        summed = recv_plane[layer, 0].astype(F32)
        for group in range(1, CHIPS):
            summed = summed + recv_plane[layer, group].astype(F32)
        for block in range(DEEP):
            send_z[layer * DEEP + block, :PIECE, :] = summed[PIECE * block : PIECE * (block + 1), :]
            send_z[layer * DEEP + block, PIECE:, :] = jnp.zeros((8 - PIECE, HALF), F32)

        @pl.loop(0, DEEP)
        def _(step):
            other = layer * DEEP + (z + step) % DEEP

            @pl.when(other != z)
            def _():
                pltpu.make_async_remote_copy(
                    src_ref=send_z.at[other], dst_ref=recv_z.at[z], send_sem=sums.at[8], recv_sem=sums.at[9],
                    device_id={"rows": other},
                ).start()

    arrange(0)
    pl.semaphore_wait(known.at[1], len(second))
    tell(known.at[2], third)
    turned_own = act1[OWN:].reshape(CELLS, C).T
    for k in range(3):
        frames = [g2[i + k, 1 : ROWS + 1] for i in range(OWN)]
        if k:
            frames = [gated(frames[i], next_mask[k][i]) for i in range(OWN)]
        part[1, k * C : (k + 1) * C] = mm(turned_own, jnp.stack(frames).reshape(CELLS, C))
    spread(0)
    arrange(1)
    arrived(g1_copy)
    dpre0[:, 1 : ROWS + 1] = (grad_of_act(g1, wtt[0]) * slope0[...]).astype(BF).reshape(OWN, ROWS, COLS, C)
    start(d_halo)
    pl.semaphore_wait(known.at[2], len(third))
    gather(0)
    spread(1)
    arrived(act_copy)
    feat_out[...] = temporal(x1[:, 2 : ROWS + 2], act1, wt[1])
    gather(1)
    recv_z[z] = send_z[z]
    arrived(d_halo)
    grad_out[...] = (
        g1[:OWN].astype(F32) + spatial_back(dpre0, wst.at[0]).reshape(OWN, ROWS, COLS, C)
    ).astype(BF)

    pltpu.make_async_remote_copy(
        src_ref=send_z.at[pl.ds(0, ZS - 1)], dst_ref=recv_z.at[pl.ds(0, ZS - 1)],
        send_sem=sums.at[8], recv_sem=sums.at[9], device_id={"rows": (z + 1) % ZS},
    ).wait()
    final = recv_z[0]
    for block in range(1, ZS):
        final = final + recv_z[block]
    total[...] = final

    for dx, dt in far_first(XS, TS):
        pltpu.make_async_remote_copy(
            src_ref=total, dst_ref=recv_all.at[place], send_sem=sums.at[10], recv_sem=sums.at[11],
            device_id=at(dx, dt, 0),
        ).start()

    recv_all[place] = final
    for group in (x_halo, x_prior, x_corner, x_handed, g_halo, g_later, g_corner, g_handed, act_copy, g1_copy, d_halo):
        sent(group)
    pltpu.make_async_remote_copy(
        src_ref=recv_all.at[pl.ds(0, PLANE - 1)], dst_ref=recv_all.at[pl.ds(0, PLANE - 1)],
        send_sem=sums.at[10], recv_sem=sums.at[11], device_id=at(1, 0, 0),
    ).wait()
    for group in range(CHIPS):
        for half in range(CORES):
            weight_out[PIECE * group : PIECE * (group + 1), HALF * half : HALF * (half + 1)] = recv_all[
                group * CORES + half, :PIECE, :
            ]


def local(clips, segment_ids, spatial_weight, temporal_weight, upstream):
    deep = PIECE * DEEP
    cells = (OWN, ROWS, COLS, C)
    anywhere = pl.BlockSpec(memory_space=pl.ANY)
    outs = (
        jax.ShapeDtypeStruct(cells, BF),
        jax.ShapeDtypeStruct(cells, BF),
        jax.ShapeDtypeStruct((6 * C // ZS, C), F32),
    )
    kept = tuple(pltpu.VMEM(out.shape, out.dtype) for out in outs)
    inside = pl.BlockSpec(memory_space=pltpu.VMEM)
    parts = pl.pallas_call(
        kernel,
        out_shape=kept,
        in_specs=[anywhere] * 5,
        out_specs=(inside,) * 3,
        scratch_shapes=[
            pltpu.VMEM((2, 3, 3, C, C), BF),
            pltpu.VMEM((2, 3, C, C), BF),
            pltpu.VMEM((2, 3, 3, C, C), BF),
            pltpu.VMEM((2, 3, C, C), BF),
            pltpu.VMEM((2 * OWN, ROWS + 6, COLS, C), BF),
            pltpu.VMEM((OWN, ROWS + 4, COLS, C), BF),
            pltpu.VMEM((2 * OWN, ROWS + 4, COLS, C), BF),
            pltpu.VMEM((2 * OWN, ROWS, COLS, C), BF),
            pltpu.VMEM((CELLS, C), F32),
            pltpu.VMEM((OWN * (ROWS + 2) * COLS, C), F32),
            pltpu.VMEM((2 * OWN, ROWS + 2, COLS, C), BF),
            pltpu.VMEM((2 * OWN, ROWS, COLS, C), BF),
            pltpu.VMEM((OWN, ROWS + 2, COLS, C), BF),
            pltpu.VMEM((OWN, ROWS + 2, COLS, C), BF),
            pltpu.VMEM((OWN * (ROWS + 2) * COLS, C), F32),
            pltpu.VMEM((C, 2 * CELLS), BF),
            pltpu.VMEM((2, 3 * C, C), F32),
            pltpu.VMEM((2, CHIPS, deep, C), F32),
            pltpu.VMEM((2, CHIPS, deep, HALF), BF),
            pltpu.VMEM((2, CHIPS, deep, HALF), BF),
            pltpu.VMEM((2, CHIPS, deep, HALF), BF),
            pltpu.VMEM((2, CHIPS, deep, HALF), BF),
            pltpu.VMEM((ZS, 8, HALF), F32),
            pltpu.VMEM((ZS, 8, HALF), F32),
            pltpu.VMEM((8, HALF), F32),
            pltpu.VMEM((PLANE, 8, HALF), F32),
            pltpu.SMEM((1, FRAMES), jnp.int32),
            pltpu.SemaphoreType.DMA((6,)),
            pltpu.SemaphoreType.DMA((14,)),
            pltpu.SemaphoreType.DMA((14,)),
            pltpu.SemaphoreType.DMA((4,)),
            pltpu.SemaphoreType.DMA((4,)),
            pltpu.SemaphoreType.DMA((12,)),
            pltpu.SemaphoreType.REGULAR((3,)),
        ],
        compiler_params=pltpu.CompilerParams(
            collective_id=0, has_side_effects=True, vmem_limit_bytes=56 * 1024 * 1024
        ),
    )(
        segment_ids,
        clips.reshape(cells),
        spatial_weight.reshape(2, 3, 3, C, C),
        temporal_weight,
        upstream.reshape(cells),
    )
    parts = [pltpu.with_memory_space_constraint(part, pltpu.VMEM) for part in parts]
    grad, features, weight_grad = pl.pallas_call(
        finish,
        out_shape=outs,
        in_specs=[inside] * 3,
        out_specs=(anywhere,) * 3,
        scratch_shapes=[pltpu.SemaphoreType.DMA((3,))],
    )(*parts)
    return (grad.reshape(clips.shape), features.reshape(clips.shape), weight_grad)


def solution(mesh):
    return jax.shard_map(
        local,
        mesh=mesh,
        in_specs=(
            P("dp", "tm", "rows", None, None),
            P("dp", None),
            P(),
            P(),
            P("dp", "tm", "rows", None, None),
        ),
        out_specs=(
            P("dp", "tm", "rows", None, None),
            P("dp", "tm", "rows", None, None),
            P("rows", None),
        ),
        check_vma=False,
    )
```

```python
import jax
import jax.numpy as jnp
from jax import lax
from jax.experimental import pallas as pl
from jax.experimental.pallas import tpu as pltpu
from jax.sharding import PartitionSpec as P

XS, YS, CORES, ZS = 4, 4, 2, 16
TS = YS * CORES
CHIPS = XS * YS
PLANE = CHIPS * CORES
PIECE = 6
HALF = 128
C = 256
COLS = 64
ROWS = 4
OWN = 2
CELLS = OWN * ROWS * COLS
FRAMES = TS * OWN
DEEP = ZS // 2
BF, F32 = jnp.bfloat16, jnp.float32


def mm(left, right):
    return jnp.dot(left, right, preferred_element_type=F32)


def rows_of(padded, first, rows):
    return padded[first : first + rows].reshape(rows * COLS, C)


def shifted(values, by):
    column = lax.broadcasted_iota(jnp.int32, values.shape, 0) % COLS
    edge = 0 if by == 1 else COLS - 1
    return jnp.where(column == edge, 0.0, pltpu.roll(values, by % values.shape[0], 0))


def spatial(padded, weights, rows):
    sums = []
    for kx in range(3):
        left = jnp.concatenate([rows_of(padded, ky, rows) for ky in range(3)], axis=1)
        right = jnp.concatenate([weights[ky, kx] for ky in range(3)], axis=0)
        sums.append(mm(left, right))
    return shifted(sums[0], 1) + sums[1] + shifted(sums[2], -1)


def spatial_back(padded, turned_weights):
    sums = []
    for kx in range(3):
        left = jnp.concatenate([rows_of(padded, 2 - ky, ROWS) for ky in range(3)], axis=1)
        right = jnp.concatenate([turned_weights[ky, kx] for ky in range(3)], axis=0)
        sums.append(mm(left, right))
    return shifted(sums[0], -1) + sums[1] + shifted(sums[2], 1)


def far_first(rows, columns):
    steps = [(i, j) for i in range(rows) for j in range(columns) if i or j]
    return sorted(steps, key=lambda step: -min(step[0], rows - step[0]) - min(step[1], columns - step[1]))


def finish(grad_in, feat_in, weight_in, grad_out, feat_out, weight_out, done):
    pairs = ((grad_in, grad_out), (feat_in, feat_out), (weight_in, weight_out))
    copies = [pltpu.make_async_copy(pair[0], pair[1], done.at[i]) for i, pair in enumerate(pairs)]
    for copy in copies:
        copy.start()
    for copy in copies:
        copy.wait()


def kernel(
    segments, clips, space_w, time_w, upstream,
    grad_out, feat_out, weight_out,
    ws, wt, wst, wtt, x0, x1, act0, act1, slope0, slope1, g2, g1, dpre1, dpre0, dact, turned, part,
    arranged, send_pair, recv_pair, send_plane, recv_plane, send_z, recv_z, total, recv_all,
    seg, load, wide_s, wide_r, near_s, near_r, sums, known,
):
    x = lax.axis_index("dp")
    t = lax.axis_index("tm")
    z = lax.axis_index("rows")
    core = t % CORES
    chip = x * YS + t // CORES
    place = x * TS + t

    def at(dx, dt, dz):
        return {"dp": (x + dx) % XS, "tm": (t + dt) % TS, "rows": (z + dz) % ZS}

    near = [(0, dt, dz) for dt in (-1, 0, 1) for dz in (-1, 0, 1) if dt or dz]
    near += [(-1, 0, 0), (1, 0, 0), (0, -2, 0), (0, 2, 0)]
    second = [(0, 0, -2), (0, 0, 2), (-1, 0, 0), (1, 0, 0), (2, 0, 0)]
    third = [(0, 0, -4), (0, 0, 4)]

    def tell(semaphore, partners):
        for partner in partners:
            pl.semaphore_signal(semaphore, inc=1, device_id=at(*partner))

    barrier = pltpu.get_barrier_semaphore()
    tell(barrier, near)

    loads = [
        pltpu.make_async_copy(clips, x0.at[pl.ds(OWN, OWN), pl.ds(3, ROWS)], load.at[0]),
        pltpu.make_async_copy(space_w.at[0], ws.at[0], load.at[1]),
        pltpu.make_async_copy(time_w, wt, load.at[2]),
        pltpu.make_async_copy(upstream, g2.at[pl.ds(0, OWN), pl.ds(1, ROWS)], load.at[3]),
        pltpu.make_async_copy(space_w.at[1], ws.at[1], load.at[4]),
        pltpu.make_async_copy(segments, seg, load.at[5]),
    ]
    for copy in loads:
        copy.start()

    def blank(ref):
        ref[...] = jnp.zeros(ref.shape, ref.dtype)

    first, last = z == 0, z == ZS - 1
    early, late = t == 0, t == TS - 1

    @pl.when(first)
    def _():
        blank(x0.at[:, pl.ds(0, 3)])
        blank(g2.at[:, pl.ds(0, 1)])
        blank(dpre0.at[:, pl.ds(0, 1)])

    @pl.when(last)
    def _():
        blank(x0.at[:, pl.ds(ROWS + 3, 3)])
        blank(g2.at[:, pl.ds(ROWS + 1, 1)])
        blank(dpre0.at[:, pl.ds(ROWS + 1, 1)])

    @pl.when(early)
    def _():
        blank(x0.at[pl.ds(0, OWN)])
        blank(act1.at[pl.ds(0, OWN)])

    @pl.when(late)
    def _():
        blank(g2.at[pl.ds(OWN, OWN)])
        blank(g1.at[pl.ds(OWN, OWN)])

    def remote(source, target, sems_s, sems_r, number, dt, dz, only=None, edge=0):
        copy = pltpu.make_async_remote_copy(
            src_ref=source, dst_ref=target, send_sem=sems_s.at[number], recv_sem=sems_r.at[number],
            device_id=at(0, dt, dz),
        )
        sends, takes = [], []
        if dt == 1:
            sends.append(t < TS - 1)
            takes.append(t > 0)
        if dt == -1:
            sends.append(t > 0)
            takes.append(t < TS - 1)
        if dz == 1:
            sends.append(z < ZS - 1)
            takes.append(z > 0)
        if dz == -1:
            sends.append(z > 0)
            takes.append(z < ZS - 1)
        if edge:
            inside = z > 0 if edge < 0 else z < ZS - 1
            sends.append(inside)
            takes.append(inside)
        if only is not None:
            sends.append(only)
            takes.append(jnp.logical_not(only))
        send, take = sends[0], takes[0]
        for more in sends[1:]:
            send = send & more
        for more in takes[1:]:
            take = take & more
        return copy, send, take

    def start(group):
        for copy, send, _ in group:
            pl.when(send)(copy.start)

    def arrived(group):
        for copy, _, take in group:
            pl.when(take)(copy.wait_recv)

    def sent(group):
        for copy, send, _ in group:
            pl.when(send)(copy.wait_send)

    x_low, x_high = clips.at[:, pl.ds(0, 3)], clips.at[:, pl.ds(1, 3)]
    prior, own = pl.ds(0, OWN), pl.ds(OWN, OWN)
    top, middle, bottom = pl.ds(0, 3), pl.ds(3, ROWS), pl.ds(ROWS + 3, 3)
    x_halo = [
        remote(x_high, x0.at[own, top], wide_s, wide_r, 0, 0, 1),
        remote(x_low, x0.at[own, bottom], wide_s, wide_r, 1, 0, -1),
    ]
    x_prior = [remote(clips, x0.at[prior, middle], wide_s, wide_r, 2, 1, 0)]
    x_corner = [
        remote(x_high, x0.at[prior, top], wide_s, wide_r, 3, 1, 1, core == 1),
        remote(x_low, x0.at[prior, bottom], wide_s, wide_r, 4, 1, -1, core == 1),
    ]
    x_handed = [
        remote(x0.at[own, top], x0.at[prior, top], wide_s, wide_r, 10, 1, 0, core == 0, -1),
        remote(x0.at[own, bottom], x0.at[prior, bottom], wide_s, wide_r, 11, 1, 0, core == 0, 1),
    ]
    g_low, g_high = upstream.at[:, pl.ds(0, 1)], upstream.at[:, pl.ds(ROWS - 1, 1)]
    now, after = pl.ds(0, OWN), pl.ds(OWN, OWN)
    over, inner, under = pl.ds(0, 1), pl.ds(1, ROWS), pl.ds(ROWS + 1, 1)
    g_halo = [
        remote(g_high, g2.at[now, over], wide_s, wide_r, 5, 0, 1),
        remote(g_low, g2.at[now, under], wide_s, wide_r, 6, 0, -1),
    ]
    g_later = [remote(upstream, g2.at[after, inner], wide_s, wide_r, 7, -1, 0)]
    g_corner = [
        remote(g_high, g2.at[after, over], wide_s, wide_r, 8, -1, 1, core == 0),
        remote(g_low, g2.at[after, under], wide_s, wide_r, 9, -1, -1, core == 0),
    ]
    g_handed = [
        remote(g2.at[now, over], g2.at[after, over], wide_s, wide_r, 12, -1, 0, core == 1, -1),
        remote(g2.at[now, under], g2.at[after, under], wide_s, wide_r, 13, -1, 0, core == 1, 1),
    ]
    act_copy = [remote(act1.at[own], act1.at[prior], near_s, near_r, 0, 1, 0)]
    g1_copy = [remote(g1.at[now], g1.at[after], near_s, near_r, 1, -1, 0)]
    d_halo = [
        remote(dpre0.at[:, pl.ds(ROWS, 1)], dpre0.at[:, over], near_s, near_r, 2, 0, 1),
        remote(dpre0.at[:, pl.ds(1, 1)], dpre0.at[:, under], near_s, near_r, 3, 0, -1),
    ]

    def gated(values, mask):
        return values * mask.astype(BF)

    def temporal(base, acts, weights, i):
        columns = []
        for k in range(3):
            frame = acts[OWN + i - k]
            if k:
                frame = gated(frame, back_mask(k, i))
            columns.append(frame.reshape(base.shape[0] * COLS, C))
        out = mm(jnp.concatenate(columns, axis=1), weights.reshape(3 * C, C))
        return (base.astype(F32) + out.reshape(base.shape)).astype(BF)

    def lifted(grads, k, rows):
        frames = [grads[i + k, rows] for i in range(OWN)]
        if k:
            frames = [gated(frames[i], next_mask(k, i)) for i in range(OWN)]
        return jnp.stack(frames).reshape(OWN * frames[0].shape[0] * COLS, C)

    def grad_of_act(grads, turned_weights, rows):
        left = jnp.concatenate([lifted(grads, k, rows) for k in range(3)], axis=1)
        return mm(left, turned_weights.reshape(3 * C, C))

    def slope(pre, sigma):
        return sigma * (1.0 + pre * (1.0 - sigma))

    pl.semaphore_wait(barrier, len(near))
    start(x_halo)
    start(x_prior)
    start(x_corner)
    start(g_later)
    tell(known.at[0], near)

    for copy in loads:
        copy.wait()

    def one_clip(frame, offset):
        before = jnp.maximum(frame - offset, 0)
        same = (frame - offset >= 0) & (frame < FRAMES) & (seg[0, before] == seg[0, jnp.minimum(frame, FRAMES - 1)])
        return jnp.where(same, 1.0, 0.0)

    first_frame = t * OWN

    def back_mask(k, i):
        return one_clip(first_frame + i, k)

    def next_mask(k, i):
        return one_clip(first_frame + i + k, k)

    @pl.loop(0, 3)
    def _(index):
        for layer in range(2):
            for kx in range(3):
                wst[layer, index, kx] = ws[layer, index, kx].T
            wtt[layer, index] = wt[layer, index].T

    arrived(x_halo)
    start(x_handed)
    start(g_halo)
    start(g_corner)
    wide, tall, flat = (ROWS + 4, COLS, C), (ROWS + 2, COLS, C), (ROWS, COLS, C)

    @pl.loop(0, 2 * OWN)
    def _(step):
        frame = (step + OWN) % (2 * OWN)

        @pl.when(step == OWN)
        def _():
            pl.semaphore_wait(known.at[0], len(near))
            tell(known.at[1], second)
            arrived(g_later)
            dact[:, inner] = grad_of_act(g2, wtt[1], inner).reshape(OWN, ROWS, COLS, C)
            arrived(x_prior)
            arrived(x_corner)
            arrived(x_handed)

        pre = spatial(x0.at[frame], ws.at[0], ROWS + 4)
        sigma = jax.nn.sigmoid(pre)
        act = (pre * sigma).astype(BF).reshape(wide)
        act0[frame] = act
        turned[:, pl.ds(pl.multiple_of(frame * 256, 256), 256)] = act[2 : ROWS + 2].reshape(256, C).T

        @pl.when(step < OWN)
        def _():
            slope0[step] = slope(pre, sigma).reshape(wide)[2 : ROWS + 2]

    arrived(g_halo)
    start(g_handed)

    @pl.loop(0, OWN)
    def _(i):
        x1[i] = temporal(x0[OWN + i, 1 : ROWS + 5], act0, wt[0], i)

    @pl.when(first)
    def _():
        blank(x1.at[:, pl.ds(0, 2)])

    @pl.when(last)
    def _():
        blank(x1.at[:, pl.ds(ROWS + 2, 2)])

    @pl.loop(0, OWN)
    def _(i):
        pre = spatial(x1.at[i], ws.at[1], ROWS + 2)
        sigma = jax.nn.sigmoid(pre)
        act1[OWN + i] = (pre * sigma).astype(BF).reshape(tall)[1 : ROWS + 1]
        slope1[i] = slope(pre, sigma).reshape(tall)

    start(act_copy)
    arrived(g_corner)
    arrived(g_handed)
    for edge in (over, under):
        dact[:, edge] = grad_of_act(g2, wtt[1], edge).reshape(OWN, 1, COLS, C)
    dpre1[...] = (dact[...] * slope1[...]).astype(BF)

    @pl.when(first)
    def _():
        blank(dpre1.at[:, over])

    @pl.when(last)
    def _():
        blank(dpre1.at[:, under])

    @pl.loop(0, OWN)
    def _(i):
        back = spatial_back(dpre1.at[i], wst.at[1]).reshape(flat)
        g1[i] = (g2[i, 1 : ROWS + 1].astype(F32) + back).astype(BF)

    start(g1_copy)
    for k in range(3):
        frames = [g1[i] for i in range(OWN)]
        if k:
            frames = [gated(frames[i], back_mask(k, i)) for i in range(OWN)]
        part[0, k * C : (k + 1) * C] = mm(
            turned[:, (OWN - k) * 256 : (2 * OWN - k) * 256], jnp.stack(frames).reshape(CELLS, C)
        )

    def pair_copy(layer):
        return pltpu.make_async_remote_copy(
            src_ref=send_pair.at[layer], dst_ref=recv_pair.at[layer], send_sem=sums.at[layer],
            recv_sem=sums.at[2 + layer], device_id={"tm": t + 1 - 2 * core},
        )

    def arrange(layer):
        @pl.loop(0, XS)
        def _(high):
            for block in range(DEEP):
                rows = part[layer, pl.ds(pl.multiple_of(96 * block + PIECE * YS * high, 8), PIECE * YS), :]
                for low in range(YS):
                    arranged[layer, high * YS + low, PIECE * block : PIECE * (block + 1), :] = rows[
                        PIECE * low : PIECE * (low + 1)
                    ]

        @pl.loop(0, CHIPS)
        def _(group):
            rows = arranged[layer, group]
            send_pair[layer, group] = jnp.where(core == 0, rows[:, HALF:], rows[:, :HALF]).astype(BF)

        pair_copy(layer).start()

    def spread(layer):
        pair_copy(layer).wait()

        @pl.loop(0, CHIPS)
        def _(group):
            rows = arranged[layer, group]
            mine = jnp.where(core == 0, rows[:, :HALF], rows[:, HALF:])
            send_plane[layer, group] = (mine + recv_pair[layer, group].astype(F32)).astype(BF)

        for dx, dy in far_first(XS, YS):
            target = at(dx, CORES * dy, 0)
            other = target["dp"] * YS + target["tm"] // CORES
            pltpu.make_async_remote_copy(
                src_ref=send_plane.at[layer, other], dst_ref=recv_plane.at[layer, chip],
                send_sem=sums.at[4 + layer], recv_sem=sums.at[6 + layer], device_id=target,
            ).start()

        recv_plane[layer, chip] = send_plane[layer, chip]

    def gather(layer):
        pltpu.make_async_remote_copy(
            src_ref=send_plane.at[layer, pl.ds(0, CHIPS - 1)], dst_ref=recv_plane.at[layer, pl.ds(0, CHIPS - 1)],
            send_sem=sums.at[4 + layer], recv_sem=sums.at[6 + layer], device_id=at(1, 0, 0),
        ).wait()
        summed = recv_plane[layer, 0].astype(F32)
        for group in range(1, CHIPS):
            summed = summed + recv_plane[layer, group].astype(F32)
        for block in range(DEEP):
            send_z[layer * DEEP + block, :PIECE, :] = summed[PIECE * block : PIECE * (block + 1), :]
            send_z[layer * DEEP + block, PIECE:, :] = jnp.zeros((8 - PIECE, HALF), F32)

        @pl.loop(0, DEEP)
        def _(step):
            other = layer * DEEP + (z + step) % DEEP

            @pl.when(other != z)
            def _():
                pltpu.make_async_remote_copy(
                    src_ref=send_z.at[other], dst_ref=recv_z.at[z], send_sem=sums.at[8], recv_sem=sums.at[9],
                    device_id={"rows": other},
                ).start()

    arrange(0)
    pl.semaphore_wait(known.at[1], len(second))
    tell(known.at[2], third)
    turned_own = act1[OWN:].reshape(CELLS, C).T
    for k in range(3):
        frames = [g2[i + k, 1 : ROWS + 1] for i in range(OWN)]
        if k:
            frames = [gated(frames[i], next_mask(k, i)) for i in range(OWN)]
        part[1, k * C : (k + 1) * C] = mm(turned_own, jnp.stack(frames).reshape(CELLS, C))
    spread(0)
    arrange(1)
    arrived(g1_copy)
    dpre0[:, 1 : ROWS + 1] = (grad_of_act(g1, wtt[0], pl.ds(0, ROWS)) * slope0[...].reshape(CELLS, C)).astype(BF).reshape(OWN, ROWS, COLS, C)
    start(d_halo)
    pl.semaphore_wait(known.at[2], len(third))
    gather(0)
    spread(1)
    arrived(act_copy)

    @pl.loop(0, OWN)
    def _(i):
        feat_out[i] = temporal(x1[i, 2 : ROWS + 2], act1, wt[1], i)

    gather(1)
    recv_z[z] = send_z[z]
    arrived(d_halo)

    @pl.loop(0, OWN)
    def _(i):
        grad_out[i] = (g1[i].astype(F32) + spatial_back(dpre0.at[i], wst.at[0]).reshape(flat)).astype(BF)

    pltpu.make_async_remote_copy(
        src_ref=send_z.at[pl.ds(0, ZS - 1)], dst_ref=recv_z.at[pl.ds(0, ZS - 1)],
        send_sem=sums.at[8], recv_sem=sums.at[9], device_id={"rows": (z + 1) % ZS},
    ).wait()
    final = recv_z[0]
    for block in range(1, ZS):
        final = final + recv_z[block]
    total[...] = final

    for dx, dt in far_first(XS, TS):
        pltpu.make_async_remote_copy(
            src_ref=total, dst_ref=recv_all.at[place], send_sem=sums.at[10], recv_sem=sums.at[11],
            device_id=at(dx, dt, 0),
        ).start()

    recv_all[place] = final
    for group in (x_halo, x_prior, x_corner, x_handed, g_halo, g_later, g_corner, g_handed, act_copy, g1_copy, d_halo):
        sent(group)
    pltpu.make_async_remote_copy(
        src_ref=recv_all.at[pl.ds(0, PLANE - 1)], dst_ref=recv_all.at[pl.ds(0, PLANE - 1)],
        send_sem=sums.at[10], recv_sem=sums.at[11], device_id=at(1, 0, 0),
    ).wait()
    for group in range(CHIPS):
        for half in range(CORES):
            weight_out[PIECE * group : PIECE * (group + 1), HALF * half : HALF * (half + 1)] = recv_all[
                group * CORES + half, :PIECE, :
            ]


def local(clips, segment_ids, spatial_weight, temporal_weight, upstream):
    deep = PIECE * DEEP
    cells = (OWN, ROWS, COLS, C)
    anywhere = pl.BlockSpec(memory_space=pl.ANY)
    outs = (
        jax.ShapeDtypeStruct(cells, BF),
        jax.ShapeDtypeStruct(cells, BF),
        jax.ShapeDtypeStruct((6 * C // ZS, C), F32),
    )
    kept = tuple(pltpu.VMEM(out.shape, out.dtype) for out in outs)
    inside = pl.BlockSpec(memory_space=pltpu.VMEM)
    parts = pl.pallas_call(
        kernel,
        out_shape=kept,
        in_specs=[anywhere] * 5,
        out_specs=(inside,) * 3,
        scratch_shapes=[
            pltpu.VMEM((2, 3, 3, C, C), BF),
            pltpu.VMEM((2, 3, C, C), BF),
            pltpu.VMEM((2, 3, 3, C, C), BF),
            pltpu.VMEM((2, 3, C, C), BF),
            pltpu.VMEM((2 * OWN, ROWS + 6, COLS, C), BF),
            pltpu.VMEM((OWN, ROWS + 4, COLS, C), BF),
            pltpu.VMEM((2 * OWN, ROWS + 4, COLS, C), BF),
            pltpu.VMEM((2 * OWN, ROWS, COLS, C), BF),
            pltpu.VMEM((OWN, ROWS, COLS, C), F32),
            pltpu.VMEM((OWN, ROWS + 2, COLS, C), F32),
            pltpu.VMEM((2 * OWN, ROWS + 2, COLS, C), BF),
            pltpu.VMEM((2 * OWN, ROWS, COLS, C), BF),
            pltpu.VMEM((OWN, ROWS + 2, COLS, C), BF),
            pltpu.VMEM((OWN, ROWS + 2, COLS, C), BF),
            pltpu.VMEM((OWN, ROWS + 2, COLS, C), F32),
            pltpu.VMEM((C, 2 * CELLS), BF),
            pltpu.VMEM((2, 3 * C, C), F32),
            pltpu.VMEM((2, CHIPS, deep, C), F32),
            pltpu.VMEM((2, CHIPS, deep, HALF), BF),
            pltpu.VMEM((2, CHIPS, deep, HALF), BF),
            pltpu.VMEM((2, CHIPS, deep, HALF), BF),
            pltpu.VMEM((2, CHIPS, deep, HALF), BF),
            pltpu.VMEM((ZS, 8, HALF), F32),
            pltpu.VMEM((ZS, 8, HALF), F32),
            pltpu.VMEM((8, HALF), F32),
            pltpu.VMEM((PLANE, 8, HALF), F32),
            pltpu.SMEM((1, FRAMES), jnp.int32),
            pltpu.SemaphoreType.DMA((6,)),
            pltpu.SemaphoreType.DMA((14,)),
            pltpu.SemaphoreType.DMA((14,)),
            pltpu.SemaphoreType.DMA((4,)),
            pltpu.SemaphoreType.DMA((4,)),
            pltpu.SemaphoreType.DMA((12,)),
            pltpu.SemaphoreType.REGULAR((3,)),
        ],
        compiler_params=pltpu.CompilerParams(
            collective_id=0, has_side_effects=True, vmem_limit_bytes=56 * 1024 * 1024
        ),
    )(
        segment_ids,
        clips.reshape(cells),
        spatial_weight.reshape(2, 3, 3, C, C),
        temporal_weight,
        upstream.reshape(cells),
    )
    parts = [pltpu.with_memory_space_constraint(part, pltpu.VMEM) for part in parts]
    grad, features, weight_grad = pl.pallas_call(
        finish,
        out_shape=outs,
        in_specs=[inside] * 3,
        out_specs=(anywhere,) * 3,
        scratch_shapes=[pltpu.SemaphoreType.DMA((3,))],
    )(*parts)
    return (grad.reshape(clips.shape), features.reshape(clips.shape), weight_grad)


def solution(mesh):
    return jax.shard_map(
        local,
        mesh=mesh,
        in_specs=(
            P("dp", "tm", "rows", None, None),
            P("dp", None),
            P(),
            P(),
            P("dp", "tm", "rows", None, None),
        ),
        out_specs=(
            P("dp", "tm", "rows", None, None),
            P("dp", "tm", "rows", None, None),
            P("rows", None),
        ),
        check_vma=False,
    )
```

```python
import jax
import jax.numpy as jnp
from jax import lax
from jax.experimental import pallas as pl
from jax.experimental.pallas import tpu as pltpu
from jax.sharding import PartitionSpec as P

XS, YS, CORES, ZS = 4, 4, 2, 16
TS = YS * CORES
CHIPS = XS * YS
PLANE = CHIPS * CORES
PIECE = 6
HALF = 128
C = 256
COLS = 64
ROWS = 4
OWN = 2
CELLS = OWN * ROWS * COLS
FRAMES = TS * OWN
DEEP = ZS // 2
BF, F32 = jnp.bfloat16, jnp.float32


def mm(left, right):
    return jnp.dot(left, right, preferred_element_type=F32)


def rows_of(padded, first, rows):
    return padded[first : first + rows].reshape(rows * COLS, C)


def shifted(values, by):
    column = lax.broadcasted_iota(jnp.int32, values.shape, 0) % COLS
    edge = 0 if by == 1 else COLS - 1
    return jnp.where(column == edge, 0.0, pltpu.roll(values, by % values.shape[0], 0))


def spatial(padded, weights, rows):
    sums = []
    for kx in range(3):
        left = jnp.concatenate([rows_of(padded, ky, rows) for ky in range(3)], axis=1)
        right = jnp.concatenate([weights[ky, kx] for ky in range(3)], axis=0)
        sums.append(mm(left, right))
    return shifted(sums[0], 1) + sums[1] + shifted(sums[2], -1)


def spatial_back(padded, turned_weights):
    sums = []
    for kx in range(3):
        left = jnp.concatenate([rows_of(padded, 2 - ky, ROWS) for ky in range(3)], axis=1)
        right = jnp.concatenate([turned_weights[ky, kx] for ky in range(3)], axis=0)
        sums.append(mm(left, right))
    return shifted(sums[0], -1) + sums[1] + shifted(sums[2], 1)


def far_first(rows, columns):
    steps = [(i, j) for i in range(rows) for j in range(columns) if i or j]
    return sorted(steps, key=lambda step: -min(step[0], rows - step[0]) - min(step[1], columns - step[1]))


def finish(grad_in, feat_in, weight_in, grad_out, feat_out, weight_out, done):
    pairs = ((grad_in, grad_out), (feat_in, feat_out), (weight_in, weight_out))
    copies = [pltpu.make_async_copy(pair[0], pair[1], done.at[i]) for i, pair in enumerate(pairs)]
    for copy in copies:
        copy.start()
    for copy in copies:
        copy.wait()


def kernel(
    segments, clips, space_w, time_w, upstream,
    grad_out, feat_out, weight_out,
    ws, wt, wst, wtt, x0, x1, act0, act1, slope0, slope1, g2, g1, dpre1, dpre0, dact, turned, part,
    arranged, send_pair, recv_pair, send_plane, recv_plane, send_z, recv_z, total, recv_all,
    seg, load, wide_s, wide_r, near_s, near_r, sums, known,
):
    x = lax.axis_index("dp")
    t = lax.axis_index("tm")
    z = lax.axis_index("rows")
    core = t % CORES
    chip = x * YS + t // CORES
    place = x * TS + t

    def at(dx, dt, dz):
        return {"dp": (x + dx) % XS, "tm": (t + dt) % TS, "rows": (z + dz) % ZS}

    near = [(0, dt, dz) for dt in (-1, 0, 1) for dz in (-1, 0, 1) if dt or dz]
    near += [(-1, 0, 0), (1, 0, 0), (0, -2, 0), (0, 2, 0)]
    second = [(0, 0, -2), (0, 0, 2), (-1, 0, 0), (1, 0, 0), (2, 0, 0)]
    third = [(0, 0, -4), (0, 0, 4)]

    def tell(semaphore, partners):
        for partner in partners:
            pl.semaphore_signal(semaphore, inc=1, device_id=at(*partner))

    barrier = pltpu.get_barrier_semaphore()
    tell(barrier, near)

    loads = [
        pltpu.make_async_copy(clips, x0.at[pl.ds(OWN, OWN), pl.ds(3, ROWS)], load.at[0]),
        pltpu.make_async_copy(space_w.at[0], ws.at[0], load.at[1]),
        pltpu.make_async_copy(time_w, wt, load.at[2]),
        pltpu.make_async_copy(upstream, g2.at[pl.ds(0, OWN), pl.ds(1, ROWS)], load.at[3]),
        pltpu.make_async_copy(space_w.at[1], ws.at[1], load.at[4]),
        pltpu.make_async_copy(segments, seg, load.at[5]),
    ]
    for copy in loads:
        copy.start()

    def blank(ref):
        ref[...] = jnp.zeros(ref.shape, ref.dtype)

    first, last = z == 0, z == ZS - 1
    early, late = t == 0, t == TS - 1

    @pl.when(first)
    def _():
        blank(x0.at[:, pl.ds(0, 3)])
        blank(g2.at[:, pl.ds(0, 1)])
        blank(dpre0.at[:, pl.ds(0, 1)])

    @pl.when(last)
    def _():
        blank(x0.at[:, pl.ds(ROWS + 3, 3)])
        blank(g2.at[:, pl.ds(ROWS + 1, 1)])
        blank(dpre0.at[:, pl.ds(ROWS + 1, 1)])

    @pl.when(early)
    def _():
        blank(x0.at[pl.ds(0, OWN)])
        blank(act1.at[pl.ds(0, OWN)])

    @pl.when(late)
    def _():
        blank(g2.at[pl.ds(OWN, OWN)])
        blank(g1.at[pl.ds(OWN, OWN)])

    def remote(source, target, sems_s, sems_r, number, dt, dz, only=None, edge=0):
        copy = pltpu.make_async_remote_copy(
            src_ref=source, dst_ref=target, send_sem=sems_s.at[number], recv_sem=sems_r.at[number],
            device_id=at(0, dt, dz),
        )
        sends, takes = [], []
        if dt == 1:
            sends.append(t < TS - 1)
            takes.append(t > 0)
        if dt == -1:
            sends.append(t > 0)
            takes.append(t < TS - 1)
        if dz == 1:
            sends.append(z < ZS - 1)
            takes.append(z > 0)
        if dz == -1:
            sends.append(z > 0)
            takes.append(z < ZS - 1)
        if edge:
            inside = z > 0 if edge < 0 else z < ZS - 1
            sends.append(inside)
            takes.append(inside)
        if only is not None:
            sends.append(only)
            takes.append(jnp.logical_not(only))
        send, take = sends[0], takes[0]
        for more in sends[1:]:
            send = send & more
        for more in takes[1:]:
            take = take & more
        return copy, send, take

    def start(group):
        for copy, send, _ in group:
            pl.when(send)(copy.start)

    def arrived(group):
        for copy, _, take in group:
            pl.when(take)(copy.wait_recv)

    def sent(group):
        for copy, send, _ in group:
            pl.when(send)(copy.wait_send)

    x_low, x_high = clips.at[:, pl.ds(0, 3)], clips.at[:, pl.ds(1, 3)]
    prior, own = pl.ds(0, OWN), pl.ds(OWN, OWN)
    top, middle, bottom = pl.ds(0, 3), pl.ds(3, ROWS), pl.ds(ROWS + 3, 3)
    x_halo = [
        remote(x_high, x0.at[own, top], wide_s, wide_r, 0, 0, 1),
        remote(x_low, x0.at[own, bottom], wide_s, wide_r, 1, 0, -1),
    ]
    x_prior = [remote(clips, x0.at[prior, middle], wide_s, wide_r, 2, 1, 0)]
    x_corner = [
        remote(x_high, x0.at[prior, top], wide_s, wide_r, 3, 1, 1, core == 1),
        remote(x_low, x0.at[prior, bottom], wide_s, wide_r, 4, 1, -1, core == 1),
    ]
    x_handed = [
        remote(x0.at[own, top], x0.at[prior, top], wide_s, wide_r, 10, 1, 0, core == 0, -1),
        remote(x0.at[own, bottom], x0.at[prior, bottom], wide_s, wide_r, 11, 1, 0, core == 0, 1),
    ]
    g_low, g_high = upstream.at[:, pl.ds(0, 1)], upstream.at[:, pl.ds(ROWS - 1, 1)]
    now, after = pl.ds(0, OWN), pl.ds(OWN, OWN)
    over, inner, under = pl.ds(0, 1), pl.ds(1, ROWS), pl.ds(ROWS + 1, 1)
    g_halo = [
        remote(g_high, g2.at[now, over], wide_s, wide_r, 5, 0, 1),
        remote(g_low, g2.at[now, under], wide_s, wide_r, 6, 0, -1),
    ]
    g_later = [remote(upstream, g2.at[after, inner], wide_s, wide_r, 7, -1, 0)]
    g_corner = [
        remote(g_high, g2.at[after, over], wide_s, wide_r, 8, -1, 1, core == 0),
        remote(g_low, g2.at[after, under], wide_s, wide_r, 9, -1, -1, core == 0),
    ]
    g_handed = [
        remote(g2.at[now, over], g2.at[after, over], wide_s, wide_r, 12, -1, 0, core == 1, -1),
        remote(g2.at[now, under], g2.at[after, under], wide_s, wide_r, 13, -1, 0, core == 1, 1),
    ]
    act_copy = [remote(act1.at[own], act1.at[prior], near_s, near_r, 0, 1, 0)]
    g1_copy = [remote(g1.at[now], g1.at[after], near_s, near_r, 1, -1, 0)]
    d_halo = [
        remote(dpre0.at[:, pl.ds(ROWS, 1)], dpre0.at[:, over], near_s, near_r, 2, 0, 1),
        remote(dpre0.at[:, pl.ds(1, 1)], dpre0.at[:, under], near_s, near_r, 3, 0, -1),
    ]

    def gated(values, mask):
        return values * mask.astype(BF)

    def temporal(base, acts, weights, i):
        columns = []
        for k in range(3):
            frame = acts[OWN + i - k]
            if k:
                frame = gated(frame, back_mask(k, i))
            columns.append(frame.reshape(base.shape[0] * COLS, C))
        out = mm(jnp.concatenate(columns, axis=1), weights.reshape(3 * C, C))
        return (base.astype(F32) + out.reshape(base.shape)).astype(BF)

    def lifted(grads, k, rows):
        frames = [grads[i + k, rows] for i in range(OWN)]
        if k:
            frames = [gated(frames[i], next_mask(k, i)) for i in range(OWN)]
        return jnp.stack(frames).reshape(OWN * frames[0].shape[0] * COLS, C)

    def grad_of_act(grads, turned_weights, rows):
        left = jnp.concatenate([lifted(grads, k, rows) for k in range(3)], axis=1)
        return mm(left, turned_weights.reshape(3 * C, C))

    def slope(pre, sigma):
        return sigma * (1.0 + pre * (1.0 - sigma))

    pl.semaphore_wait(barrier, len(near))
    pl.when(core == 0)(lambda: start(x_halo))
    start(x_corner)
    start(x_prior)
    start(g_later)
    tell(known.at[0], near)

    for copy in loads:
        copy.wait()

    def one_clip(frame, offset):
        before = jnp.maximum(frame - offset, 0)
        same = (frame - offset >= 0) & (frame < FRAMES) & (seg[0, before] == seg[0, jnp.minimum(frame, FRAMES - 1)])
        return jnp.where(same, 1.0, 0.0)

    first_frame = t * OWN

    def back_mask(k, i):
        return one_clip(first_frame + i, k)

    def next_mask(k, i):
        return one_clip(first_frame + i + k, k)

    @pl.loop(0, 3)
    def _(index):
        for layer in range(2):
            for kx in range(3):
                wst[layer, index, kx] = ws[layer, index, kx].T
            wtt[layer, index] = wt[layer, index].T

    pl.when(core == 1)(lambda: start(x_halo))

    arrived(x_halo)
    start(x_handed)
    start(g_halo)
    start(g_corner)
    wide, tall, flat = (ROWS + 4, COLS, C), (ROWS + 2, COLS, C), (ROWS, COLS, C)

    @pl.loop(0, 2 * OWN)
    def _(step):
        frame = (step + OWN) % (2 * OWN)

        @pl.when(step == OWN)
        def _():
            pl.semaphore_wait(known.at[0], len(near))
            tell(known.at[1], second)
            arrived(g_later)
            dact[:, inner] = grad_of_act(g2, wtt[1], inner).reshape(OWN, ROWS, COLS, C)
            arrived(x_prior)
            arrived(x_corner)
            arrived(x_handed)

        pre = spatial(x0.at[frame], ws.at[0], ROWS + 4)
        sigma = jax.nn.sigmoid(pre)
        act = (pre * sigma).astype(BF).reshape(wide)
        act0[frame] = act
        turned[:, pl.ds(pl.multiple_of(frame * 256, 256), 256)] = act[2 : ROWS + 2].reshape(256, C).T

        @pl.when(step < OWN)
        def _():
            slope0[step] = slope(pre, sigma).reshape(wide)[2 : ROWS + 2]

    arrived(g_halo)
    start(g_handed)

    @pl.loop(0, OWN)
    def _(i):
        x1[i] = temporal(x0[OWN + i, 1 : ROWS + 5], act0, wt[0], i)

    @pl.when(first)
    def _():
        blank(x1.at[:, pl.ds(0, 2)])

    @pl.when(last)
    def _():
        blank(x1.at[:, pl.ds(ROWS + 2, 2)])

    @pl.loop(0, OWN)
    def _(i):
        pre = spatial(x1.at[i], ws.at[1], ROWS + 2)
        sigma = jax.nn.sigmoid(pre)
        act1[OWN + i] = (pre * sigma).astype(BF).reshape(tall)[1 : ROWS + 1]
        slope1[i] = slope(pre, sigma).reshape(tall)

    start(act_copy)
    arrived(g_corner)
    arrived(g_handed)
    for edge in (over, under):
        dact[:, edge] = grad_of_act(g2, wtt[1], edge).reshape(OWN, 1, COLS, C)
    dpre1[...] = (dact[...] * slope1[...]).astype(BF)

    @pl.when(first)
    def _():
        blank(dpre1.at[:, over])

    @pl.when(last)
    def _():
        blank(dpre1.at[:, under])

    @pl.loop(0, OWN)
    def _(i):
        back = spatial_back(dpre1.at[i], wst.at[1]).reshape(flat)
        g1[i] = (g2[i, 1 : ROWS + 1].astype(F32) + back).astype(BF)

    start(g1_copy)
    for k in range(3):
        frames = [g1[i] for i in range(OWN)]
        if k:
            frames = [gated(frames[i], back_mask(k, i)) for i in range(OWN)]
        part[0, k * C : (k + 1) * C] = mm(
            turned[:, (OWN - k) * 256 : (2 * OWN - k) * 256], jnp.stack(frames).reshape(CELLS, C)
        )

    def pair_copy(layer):
        return pltpu.make_async_remote_copy(
            src_ref=send_pair.at[layer], dst_ref=recv_pair.at[layer], send_sem=sums.at[layer],
            recv_sem=sums.at[2 + layer], device_id={"tm": t + 1 - 2 * core},
        )

    def arrange(layer):
        @pl.loop(0, XS)
        def _(high):
            for block in range(DEEP):
                rows = part[layer, pl.ds(pl.multiple_of(96 * block + PIECE * YS * high, 8), PIECE * YS), :]
                for low in range(YS):
                    arranged[layer, high * YS + low, PIECE * block : PIECE * (block + 1), :] = rows[
                        PIECE * low : PIECE * (low + 1)
                    ]

        @pl.loop(0, CHIPS)
        def _(group):
            rows = arranged[layer, group]
            send_pair[layer, group] = jnp.where(core == 0, rows[:, HALF:], rows[:, :HALF]).astype(BF)

        pair_copy(layer).start()

    def spread(layer):
        pair_copy(layer).wait()

        @pl.loop(0, CHIPS)
        def _(group):
            rows = arranged[layer, group]
            mine = jnp.where(core == 0, rows[:, :HALF], rows[:, HALF:])
            send_plane[layer, group] = (mine + recv_pair[layer, group].astype(F32)).astype(BF)

        for dx, dy in far_first(XS, YS):
            target = at(dx, CORES * dy, 0)
            other = target["dp"] * YS + target["tm"] // CORES
            pltpu.make_async_remote_copy(
                src_ref=send_plane.at[layer, other], dst_ref=recv_plane.at[layer, chip],
                send_sem=sums.at[4 + layer], recv_sem=sums.at[6 + layer], device_id=target,
            ).start()

        recv_plane[layer, chip] = send_plane[layer, chip]

    def gather(layer):
        pltpu.make_async_remote_copy(
            src_ref=send_plane.at[layer, pl.ds(0, CHIPS - 1)], dst_ref=recv_plane.at[layer, pl.ds(0, CHIPS - 1)],
            send_sem=sums.at[4 + layer], recv_sem=sums.at[6 + layer], device_id=at(1, 0, 0),
        ).wait()
        summed = recv_plane[layer, 0].astype(F32)
        for group in range(1, CHIPS):
            summed = summed + recv_plane[layer, group].astype(F32)
        for block in range(DEEP):
            send_z[layer * DEEP + block, :PIECE, :] = summed[PIECE * block : PIECE * (block + 1), :]
            send_z[layer * DEEP + block, PIECE:, :] = jnp.zeros((8 - PIECE, HALF), F32)

        @pl.loop(0, DEEP)
        def _(step):
            other = layer * DEEP + (z + step) % DEEP

            @pl.when(other != z)
            def _():
                pltpu.make_async_remote_copy(
                    src_ref=send_z.at[other], dst_ref=recv_z.at[z], send_sem=sums.at[8], recv_sem=sums.at[9],
                    device_id={"rows": other},
                ).start()

    arrange(0)
    pl.semaphore_wait(known.at[1], len(second))
    tell(known.at[2], third)
    turned_own = act1[OWN:].reshape(CELLS, C).T
    for k in range(3):
        frames = [g2[i + k, 1 : ROWS + 1] for i in range(OWN)]
        if k:
            frames = [gated(frames[i], next_mask(k, i)) for i in range(OWN)]
        part[1, k * C : (k + 1) * C] = mm(turned_own, jnp.stack(frames).reshape(CELLS, C))
    spread(0)
    arrange(1)
    arrived(g1_copy)
    dpre0[:, 1 : ROWS + 1] = (grad_of_act(g1, wtt[0], pl.ds(0, ROWS)) * slope0[...].reshape(CELLS, C)).astype(BF).reshape(OWN, ROWS, COLS, C)
    start(d_halo)
    pl.semaphore_wait(known.at[2], len(third))
    gather(0)
    spread(1)
    arrived(act_copy)

    @pl.loop(0, OWN)
    def _(i):
        feat_out[i] = temporal(x1[i, 2 : ROWS + 2], act1, wt[1], i)

    gather(1)
    recv_z[z] = send_z[z]
    arrived(d_halo)

    @pl.loop(0, OWN)
    def _(i):
        grad_out[i] = (g1[i].astype(F32) + spatial_back(dpre0.at[i], wst.at[0]).reshape(flat)).astype(BF)

    pltpu.make_async_remote_copy(
        src_ref=send_z.at[pl.ds(0, ZS - 1)], dst_ref=recv_z.at[pl.ds(0, ZS - 1)],
        send_sem=sums.at[8], recv_sem=sums.at[9], device_id={"rows": (z + 1) % ZS},
    ).wait()
    final = recv_z[0]
    for block in range(1, ZS):
        final = final + recv_z[block]
    total[...] = final

    for dx, dt in far_first(XS, TS):
        pltpu.make_async_remote_copy(
            src_ref=total, dst_ref=recv_all.at[place], send_sem=sums.at[10], recv_sem=sums.at[11],
            device_id=at(dx, dt, 0),
        ).start()

    recv_all[place] = final
    for group in (x_halo, x_prior, x_corner, x_handed, g_halo, g_later, g_corner, g_handed, act_copy, g1_copy, d_halo):
        sent(group)
    pltpu.make_async_remote_copy(
        src_ref=recv_all.at[pl.ds(0, PLANE - 1)], dst_ref=recv_all.at[pl.ds(0, PLANE - 1)],
        send_sem=sums.at[10], recv_sem=sums.at[11], device_id=at(1, 0, 0),
    ).wait()
    for group in range(CHIPS):
        for half in range(CORES):
            weight_out[PIECE * group : PIECE * (group + 1), HALF * half : HALF * (half + 1)] = recv_all[
                group * CORES + half, :PIECE, :
            ]


def local(clips, segment_ids, spatial_weight, temporal_weight, upstream):
    deep = PIECE * DEEP
    cells = (OWN, ROWS, COLS, C)
    anywhere = pl.BlockSpec(memory_space=pl.ANY)
    outs = (
        jax.ShapeDtypeStruct(cells, BF),
        jax.ShapeDtypeStruct(cells, BF),
        jax.ShapeDtypeStruct((6 * C // ZS, C), F32),
    )
    kept = tuple(pltpu.VMEM(out.shape, out.dtype) for out in outs)
    inside = pl.BlockSpec(memory_space=pltpu.VMEM)
    parts = pl.pallas_call(
        kernel,
        out_shape=kept,
        in_specs=[anywhere] * 5,
        out_specs=(inside,) * 3,
        scratch_shapes=[
            pltpu.VMEM((2, 3, 3, C, C), BF),
            pltpu.VMEM((2, 3, C, C), BF),
            pltpu.VMEM((2, 3, 3, C, C), BF),
            pltpu.VMEM((2, 3, C, C), BF),
            pltpu.VMEM((2 * OWN, ROWS + 6, COLS, C), BF),
            pltpu.VMEM((OWN, ROWS + 4, COLS, C), BF),
            pltpu.VMEM((2 * OWN, ROWS + 4, COLS, C), BF),
            pltpu.VMEM((2 * OWN, ROWS, COLS, C), BF),
            pltpu.VMEM((OWN, ROWS, COLS, C), F32),
            pltpu.VMEM((OWN, ROWS + 2, COLS, C), F32),
            pltpu.VMEM((2 * OWN, ROWS + 2, COLS, C), BF),
            pltpu.VMEM((2 * OWN, ROWS, COLS, C), BF),
            pltpu.VMEM((OWN, ROWS + 2, COLS, C), BF),
            pltpu.VMEM((OWN, ROWS + 2, COLS, C), BF),
            pltpu.VMEM((OWN, ROWS + 2, COLS, C), F32),
            pltpu.VMEM((C, 2 * CELLS), BF),
            pltpu.VMEM((2, 3 * C, C), F32),
            pltpu.VMEM((2, CHIPS, deep, C), F32),
            pltpu.VMEM((2, CHIPS, deep, HALF), BF),
            pltpu.VMEM((2, CHIPS, deep, HALF), BF),
            pltpu.VMEM((2, CHIPS, deep, HALF), BF),
            pltpu.VMEM((2, CHIPS, deep, HALF), BF),
            pltpu.VMEM((ZS, 8, HALF), F32),
            pltpu.VMEM((ZS, 8, HALF), F32),
            pltpu.VMEM((8, HALF), F32),
            pltpu.VMEM((PLANE, 8, HALF), F32),
            pltpu.SMEM((1, FRAMES), jnp.int32),
            pltpu.SemaphoreType.DMA((6,)),
            pltpu.SemaphoreType.DMA((14,)),
            pltpu.SemaphoreType.DMA((14,)),
            pltpu.SemaphoreType.DMA((4,)),
            pltpu.SemaphoreType.DMA((4,)),
            pltpu.SemaphoreType.DMA((12,)),
            pltpu.SemaphoreType.REGULAR((3,)),
        ],
        compiler_params=pltpu.CompilerParams(
            collective_id=0, has_side_effects=True, vmem_limit_bytes=56 * 1024 * 1024
        ),
    )(
        segment_ids,
        clips.reshape(cells),
        spatial_weight.reshape(2, 3, 3, C, C),
        temporal_weight,
        upstream.reshape(cells),
    )
    parts = [pltpu.with_memory_space_constraint(part, pltpu.VMEM) for part in parts]
    grad, features, weight_grad = pl.pallas_call(
        finish,
        out_shape=outs,
        in_specs=[inside] * 3,
        out_specs=(anywhere,) * 3,
        scratch_shapes=[pltpu.SemaphoreType.DMA((3,))],
    )(*parts)
    return (grad.reshape(clips.shape), features.reshape(clips.shape), weight_grad)


def solution(mesh):
    return jax.shard_map(
        local,
        mesh=mesh,
        in_specs=(
            P("dp", "tm", "rows", None, None),
            P("dp", None),
            P(),
            P(),
            P("dp", "tm", "rows", None, None),
        ),
        out_specs=(
            P("dp", "tm", "rows", None, None),
            P("dp", "tm", "rows", None, None),
            P("rows", None),
        ),
        check_vma=False,
    )
```

```python
import jax
import jax.numpy as jnp
from jax import lax
from jax.experimental import pallas as pl
from jax.experimental.pallas import tpu as pltpu
from jax.sharding import PartitionSpec as P

XS, YS, CORES, ZS = 4, 4, 2, 16
TS = YS * CORES
CHIPS = XS * YS
PLANE = CHIPS * CORES
PIECE = 6
HALF = 128
C = 256
COLS = 64
ROWS = 4
OWN = 2
CELLS = OWN * ROWS * COLS
FRAMES = TS * OWN
DEEP = ZS // 2
BF, F32 = jnp.bfloat16, jnp.float32


def mm(left, right):
    return jnp.dot(left, right, preferred_element_type=F32)


def rows_of(padded, first, rows):
    return padded[first : first + rows].reshape(rows * COLS, C)


def shifted(values, by):
    column = lax.broadcasted_iota(jnp.int32, values.shape, 0) % COLS
    edge = 0 if by == 1 else COLS - 1
    return jnp.where(column == edge, 0.0, pltpu.roll(values, by % values.shape[0], 0))


def spatial(padded, weights, rows):
    sums = []
    for kx in range(3):
        left = jnp.concatenate([rows_of(padded, ky, rows) for ky in range(3)], axis=1)
        right = jnp.concatenate([weights[ky, kx] for ky in range(3)], axis=0)
        sums.append(mm(left, right))
    return shifted(sums[0], 1) + sums[1] + shifted(sums[2], -1)


def spatial_back(padded, turned_weights):
    sums = []
    for kx in range(3):
        left = jnp.concatenate([rows_of(padded, 2 - ky, ROWS) for ky in range(3)], axis=1)
        right = jnp.concatenate([turned_weights[ky, kx] for ky in range(3)], axis=0)
        sums.append(mm(left, right))
    return shifted(sums[0], -1) + sums[1] + shifted(sums[2], 1)


def far_first(rows, columns):
    steps = [(i, j) for i in range(rows) for j in range(columns) if i or j]
    return sorted(steps, key=lambda step: -min(step[0], rows - step[0]) - min(step[1], columns - step[1]))


def finish(grad_in, feat_in, weight_in, grad_out, feat_out, weight_out, done):
    pairs = ((grad_in, grad_out), (feat_in, feat_out), (weight_in, weight_out))
    copies = [pltpu.make_async_copy(pair[0], pair[1], done.at[i]) for i, pair in enumerate(pairs)]
    for copy in copies:
        copy.start()
    for copy in copies:
        copy.wait()


def kernel(
    segments, clips, space_w, time_w, upstream,
    grad_out, feat_out, weight_out,
    ws, wt, wst, wtt, x0, x1, act0, act1, slope0, slope1, g2, g1, dpre1, dpre0, dact, turned, part,
    arranged, send_pair, recv_pair, send_plane, recv_plane, send_z, recv_z, total, recv_all,
    seg, load, wide_s, wide_r, near_s, near_r, sums, known,
):
    x = lax.axis_index("dp")
    t = lax.axis_index("tm")
    z = lax.axis_index("rows")
    core = t % CORES
    chip = x * YS + t // CORES
    place = x * TS + t

    def at(dx, dt, dz):
        return {"dp": (x + dx) % XS, "tm": (t + dt) % TS, "rows": (z + dz) % ZS}

    near = [(0, dt, dz) for dt in (-1, 0, 1) for dz in (-1, 0, 1) if dt or dz]
    near += [(-1, 0, 0), (1, 0, 0), (0, -2, 0), (0, 2, 0)]
    second = [(0, 0, -2), (0, 0, 2), (-1, 0, 0), (1, 0, 0), (2, 0, 0)]
    third = [(0, 0, -4), (0, 0, 4)]

    def tell(semaphore, partners):
        for partner in partners:
            pl.semaphore_signal(semaphore, inc=1, device_id=at(*partner))

    barrier = pltpu.get_barrier_semaphore()
    tell(barrier, near)

    loads = [
        pltpu.make_async_copy(clips, x0.at[pl.ds(OWN, OWN), pl.ds(3, ROWS)], load.at[0]),
        pltpu.make_async_copy(space_w.at[0], ws.at[0], load.at[1]),
        pltpu.make_async_copy(time_w, wt, load.at[2]),
        pltpu.make_async_copy(upstream, g2.at[pl.ds(0, OWN), pl.ds(1, ROWS)], load.at[3]),
        pltpu.make_async_copy(space_w.at[1], ws.at[1], load.at[4]),
        pltpu.make_async_copy(segments, seg, load.at[5]),
    ]
    for copy in loads:
        copy.start()

    def blank(ref):
        ref[...] = jnp.zeros(ref.shape, ref.dtype)

    first, last = z == 0, z == ZS - 1
    early, late = t == 0, t == TS - 1

    @pl.when(first)
    def _():
        blank(x0.at[:, pl.ds(0, 3)])
        blank(g2.at[:, pl.ds(0, 1)])
        blank(dpre0.at[:, pl.ds(0, 1)])

    @pl.when(last)
    def _():
        blank(x0.at[:, pl.ds(ROWS + 3, 3)])
        blank(g2.at[:, pl.ds(ROWS + 1, 1)])
        blank(dpre0.at[:, pl.ds(ROWS + 1, 1)])

    @pl.when(early)
    def _():
        blank(x0.at[pl.ds(0, OWN)])
        blank(act1.at[pl.ds(0, OWN)])

    @pl.when(late)
    def _():
        blank(g2.at[pl.ds(OWN, OWN)])
        blank(g1.at[pl.ds(OWN, OWN)])

    def remote(source, target, sems_s, sems_r, number, dt, dz, only=None, edge=0):
        copy = pltpu.make_async_remote_copy(
            src_ref=source, dst_ref=target, send_sem=sems_s.at[number], recv_sem=sems_r.at[number],
            device_id=at(0, dt, dz),
        )
        sends, takes = [], []
        if dt == 1:
            sends.append(t < TS - 1)
            takes.append(t > 0)
        if dt == -1:
            sends.append(t > 0)
            takes.append(t < TS - 1)
        if dz == 1:
            sends.append(z < ZS - 1)
            takes.append(z > 0)
        if dz == -1:
            sends.append(z > 0)
            takes.append(z < ZS - 1)
        if edge:
            inside = z > 0 if edge < 0 else z < ZS - 1
            sends.append(inside)
            takes.append(inside)
        if only is not None:
            sends.append(only)
            takes.append(jnp.logical_not(only))
        send, take = sends[0], takes[0]
        for more in sends[1:]:
            send = send & more
        for more in takes[1:]:
            take = take & more
        return copy, send, take

    def start(group):
        for copy, send, _ in group:
            pl.when(send)(copy.start)

    def arrived(group):
        for copy, _, take in group:
            pl.when(take)(copy.wait_recv)

    def sent(group):
        for copy, send, _ in group:
            pl.when(send)(copy.wait_send)

    x_low, x_high = clips.at[:, pl.ds(0, 3)], clips.at[:, pl.ds(1, 3)]
    prior, own = pl.ds(0, OWN), pl.ds(OWN, OWN)
    top, middle, bottom = pl.ds(0, 3), pl.ds(3, ROWS), pl.ds(ROWS + 3, 3)
    x_halo = [
        remote(x_high, x0.at[own, top], wide_s, wide_r, 0, 0, 1),
        remote(x_low, x0.at[own, bottom], wide_s, wide_r, 1, 0, -1),
    ]
    x_prior = [remote(clips, x0.at[prior, middle], wide_s, wide_r, 2, 1, 0)]
    x_corner = [
        remote(x_high, x0.at[prior, top], wide_s, wide_r, 3, 1, 1, core == 1),
        remote(x_low, x0.at[prior, bottom], wide_s, wide_r, 4, 1, -1, core == 1),
    ]
    x_handed = [
        remote(x0.at[own, top], x0.at[prior, top], wide_s, wide_r, 10, 1, 0, core == 0, -1),
        remote(x0.at[own, bottom], x0.at[prior, bottom], wide_s, wide_r, 11, 1, 0, core == 0, 1),
    ]
    g_low, g_high = upstream.at[:, pl.ds(0, 1)], upstream.at[:, pl.ds(ROWS - 1, 1)]
    now, after = pl.ds(0, OWN), pl.ds(OWN, OWN)
    over, inner, under = pl.ds(0, 1), pl.ds(1, ROWS), pl.ds(ROWS + 1, 1)
    g_halo = [
        remote(g_high, g2.at[now, over], wide_s, wide_r, 5, 0, 1),
        remote(g_low, g2.at[now, under], wide_s, wide_r, 6, 0, -1),
    ]
    g_later = [remote(upstream, g2.at[after, inner], wide_s, wide_r, 7, -1, 0)]
    g_corner = [
        remote(g_high, g2.at[after, over], wide_s, wide_r, 8, -1, 1, core == 0),
        remote(g_low, g2.at[after, under], wide_s, wide_r, 9, -1, -1, core == 0),
    ]
    g_handed = [
        remote(g2.at[now, over], g2.at[after, over], wide_s, wide_r, 12, -1, 0, core == 1, -1),
        remote(g2.at[now, under], g2.at[after, under], wide_s, wide_r, 13, -1, 0, core == 1, 1),
    ]
    act_copy = [remote(act1.at[own], act1.at[prior], near_s, near_r, 0, 1, 0)]
    g1_copy = [remote(g1.at[now], g1.at[after], near_s, near_r, 1, -1, 0)]
    d_halo = [
        remote(dpre0.at[:, pl.ds(ROWS, 1)], dpre0.at[:, over], near_s, near_r, 2, 0, 1),
        remote(dpre0.at[:, pl.ds(1, 1)], dpre0.at[:, under], near_s, near_r, 3, 0, -1),
    ]

    def gated(values, mask):
        return values * mask.astype(BF)

    def temporal(base, acts, weights, i):
        columns = []
        for k in range(3):
            frame = acts[OWN + i - k]
            if k:
                frame = gated(frame, back_mask(k, i))
            columns.append(frame.reshape(base.shape[0] * COLS, C))
        out = mm(jnp.concatenate(columns, axis=1), weights.reshape(3 * C, C))
        return (base.astype(F32) + out.reshape(base.shape)).astype(BF)

    def lifted(grads, k, rows):
        frames = [grads[i + k, rows] for i in range(OWN)]
        if k:
            frames = [gated(frames[i], next_mask(k, i)) for i in range(OWN)]
        return jnp.stack(frames).reshape(OWN * frames[0].shape[0] * COLS, C)

    def grad_of_act(grads, turned_weights, rows):
        left = jnp.concatenate([lifted(grads, k, rows) for k in range(3)], axis=1)
        return mm(left, turned_weights.reshape(3 * C, C))

    def slope(pre, sigma):
        return sigma * (1.0 + pre * (1.0 - sigma))

    pl.semaphore_wait(barrier, len(near))
    pl.when(core == 0)(lambda: start(x_halo))
    start(x_corner)
    start(x_prior)
    start(g_later)
    tell(known.at[0], near)

    for copy in loads:
        copy.wait()

    def one_clip(frame, offset):
        before = jnp.maximum(frame - offset, 0)
        same = (frame - offset >= 0) & (frame < FRAMES) & (seg[0, before] == seg[0, jnp.minimum(frame, FRAMES - 1)])
        return jnp.where(same, 1.0, 0.0)

    first_frame = t * OWN

    def back_mask(k, i):
        return one_clip(first_frame + i, k)

    def next_mask(k, i):
        return one_clip(first_frame + i + k, k)

    @pl.loop(0, 3)
    def _(index):
        for layer in range(2):
            for kx in range(3):
                wst[layer, index, kx] = ws[layer, index, kx].T
            wtt[layer, index] = wt[layer, index].T

    pl.when(core == 1)(lambda: start(x_halo))

    arrived(x_halo)
    start(x_handed)
    start(g_halo)
    start(g_corner)
    wide, tall, flat = (ROWS + 4, COLS, C), (ROWS + 2, COLS, C), (ROWS, COLS, C)

    @pl.loop(0, 2 * OWN)
    def _(step):
        frame = (step + OWN) % (2 * OWN)

        @pl.when(step == OWN)
        def _():
            pl.semaphore_wait(known.at[0], len(near))
            tell(known.at[1], second)
            arrived(g_later)
            dact[:, inner] = grad_of_act(g2, wtt[1], inner).reshape(OWN, ROWS, COLS, C)
            arrived(x_prior)
            arrived(x_corner)
            arrived(x_handed)

        pre = spatial(x0.at[frame], ws.at[0], ROWS + 4)
        sigma = jax.nn.sigmoid(pre)
        act = (pre * sigma).astype(BF).reshape(wide)
        act0[frame] = act
        turned[:, pl.ds(pl.multiple_of(frame * 256, 256), 256)] = act[2 : ROWS + 2].reshape(256, C).T

        @pl.when(step < OWN)
        def _():
            slope0[step] = slope(pre, sigma).reshape(wide)[2 : ROWS + 2]

    arrived(g_halo)
    start(g_handed)

    @pl.loop(0, OWN)
    def _(i):
        x1[i] = temporal(x0[OWN + i, 1 : ROWS + 5], act0, wt[0], i)

    @pl.when(first)
    def _():
        blank(x1.at[:, pl.ds(0, 2)])

    @pl.when(last)
    def _():
        blank(x1.at[:, pl.ds(ROWS + 2, 2)])

    @pl.loop(0, OWN)
    def _(i):
        pre = spatial(x1.at[i], ws.at[1], ROWS + 2)
        sigma = jax.nn.sigmoid(pre)
        act1[OWN + i] = (pre * sigma).astype(BF).reshape(tall)[1 : ROWS + 1]
        slope1[i] = slope(pre, sigma).reshape(tall)

    start(act_copy)
    arrived(g_corner)
    arrived(g_handed)
    for edge in (over, under):
        dact[:, edge] = grad_of_act(g2, wtt[1], edge).reshape(OWN, 1, COLS, C)
    dpre1[...] = (dact[...] * slope1[...]).astype(BF)

    @pl.when(first)
    def _():
        blank(dpre1.at[:, over])

    @pl.when(last)
    def _():
        blank(dpre1.at[:, under])

    @pl.loop(0, OWN)
    def _(i):
        back = spatial_back(dpre1.at[i], wst.at[1]).reshape(flat)
        g1[i] = (g2[i, 1 : ROWS + 1].astype(F32) + back).astype(BF)

    start(g1_copy)
    for k in range(3):
        frames = [g1[i] for i in range(OWN)]
        if k:
            frames = [gated(frames[i], back_mask(k, i)) for i in range(OWN)]
        part[0, k * C : (k + 1) * C] = mm(
            turned[:, (OWN - k) * 256 : (2 * OWN - k) * 256], jnp.stack(frames).reshape(CELLS, C)
        )

    def pair_copy(layer):
        return pltpu.make_async_remote_copy(
            src_ref=send_pair.at[layer], dst_ref=recv_pair.at[layer], send_sem=sums.at[layer],
            recv_sem=sums.at[2 + layer], device_id={"tm": t + 1 - 2 * core},
        )

    def arrange(layer):
        @pl.loop(0, XS)
        def _(high):
            for block in range(DEEP):
                rows = part[layer, pl.ds(pl.multiple_of(96 * block + PIECE * YS * high, 8), PIECE * YS), :]
                for low in range(YS):
                    arranged[layer, high * YS + low, PIECE * block : PIECE * (block + 1), :] = rows[
                        PIECE * low : PIECE * (low + 1)
                    ]

        @pl.loop(0, CHIPS)
        def _(group):
            other = pl.ds(pl.multiple_of((1 - core) * HALF, HALF), HALF)
            send_pair[layer, group] = arranged[layer, group, :, other].astype(BF)

        pair_copy(layer).start()

    def spread(layer):
        pair_copy(layer).wait()

        @pl.loop(0, CHIPS)
        def _(group):
            mine = arranged[layer, group, :, pl.ds(pl.multiple_of(core * HALF, HALF), HALF)]
            send_plane[layer, group] = (mine + recv_pair[layer, group].astype(F32)).astype(BF)

        for dx, dy in far_first(XS, YS):
            target = at(dx, CORES * dy, 0)
            other = target["dp"] * YS + target["tm"] // CORES
            pltpu.make_async_remote_copy(
                src_ref=send_plane.at[layer, other], dst_ref=recv_plane.at[layer, chip],
                send_sem=sums.at[4 + layer], recv_sem=sums.at[6 + layer], device_id=target,
            ).start()

        recv_plane[layer, chip] = send_plane[layer, chip]

    def gather(layer):
        pltpu.make_async_remote_copy(
            src_ref=send_plane.at[layer, pl.ds(0, CHIPS - 1)], dst_ref=recv_plane.at[layer, pl.ds(0, CHIPS - 1)],
            send_sem=sums.at[4 + layer], recv_sem=sums.at[6 + layer], device_id=at(1, 0, 0),
        ).wait()
        summed = recv_plane[layer, 0].astype(F32)
        for group in range(1, CHIPS):
            summed = summed + recv_plane[layer, group].astype(F32)
        for block in range(DEEP):
            send_z[layer * DEEP + block, :PIECE, :] = summed[PIECE * block : PIECE * (block + 1), :]
            send_z[layer * DEEP + block, PIECE:, :] = jnp.zeros((8 - PIECE, HALF), F32)

        @pl.loop(0, DEEP)
        def _(step):
            other = layer * DEEP + (z + step) % DEEP

            @pl.when(other != z)
            def _():
                pltpu.make_async_remote_copy(
                    src_ref=send_z.at[other], dst_ref=recv_z.at[z], send_sem=sums.at[8], recv_sem=sums.at[9],
                    device_id={"rows": other},
                ).start()

    arrange(0)
    pl.semaphore_wait(known.at[1], len(second))
    tell(known.at[2], third)
    turned_own = act1[OWN:].reshape(CELLS, C).T
    for k in range(3):
        frames = [g2[i + k, 1 : ROWS + 1] for i in range(OWN)]
        if k:
            frames = [gated(frames[i], next_mask(k, i)) for i in range(OWN)]
        part[1, k * C : (k + 1) * C] = mm(turned_own, jnp.stack(frames).reshape(CELLS, C))
    spread(0)
    arrange(1)
    arrived(g1_copy)
    dpre0[:, 1 : ROWS + 1] = (grad_of_act(g1, wtt[0], pl.ds(0, ROWS)) * slope0[...].reshape(CELLS, C)).astype(BF).reshape(OWN, ROWS, COLS, C)
    start(d_halo)
    pl.semaphore_wait(known.at[2], len(third))
    gather(0)
    spread(1)
    arrived(act_copy)

    @pl.loop(0, OWN)
    def _(i):
        feat_out[i] = temporal(x1[i, 2 : ROWS + 2], act1, wt[1], i)

    gather(1)
    recv_z[z] = send_z[z]
    arrived(d_halo)

    @pl.loop(0, OWN)
    def _(i):
        grad_out[i] = (g1[i].astype(F32) + spatial_back(dpre0.at[i], wst.at[0]).reshape(flat)).astype(BF)

    pltpu.make_async_remote_copy(
        src_ref=send_z.at[pl.ds(0, ZS - 1)], dst_ref=recv_z.at[pl.ds(0, ZS - 1)],
        send_sem=sums.at[8], recv_sem=sums.at[9], device_id={"rows": (z + 1) % ZS},
    ).wait()
    final = recv_z[0]
    for block in range(1, ZS):
        final = final + recv_z[block]
    total[...] = final

    for dx, dt in far_first(XS, TS):
        pltpu.make_async_remote_copy(
            src_ref=total, dst_ref=recv_all.at[place], send_sem=sums.at[10], recv_sem=sums.at[11],
            device_id=at(dx, dt, 0),
        ).start()

    recv_all[place] = final
    for group in (x_halo, x_prior, x_corner, x_handed, g_halo, g_later, g_corner, g_handed, act_copy, g1_copy, d_halo):
        sent(group)
    pltpu.make_async_remote_copy(
        src_ref=recv_all.at[pl.ds(0, PLANE - 1)], dst_ref=recv_all.at[pl.ds(0, PLANE - 1)],
        send_sem=sums.at[10], recv_sem=sums.at[11], device_id=at(1, 0, 0),
    ).wait()
    for group in range(CHIPS):
        for half in range(CORES):
            weight_out[PIECE * group : PIECE * (group + 1), HALF * half : HALF * (half + 1)] = recv_all[
                group * CORES + half, :PIECE, :
            ]


def local(clips, segment_ids, spatial_weight, temporal_weight, upstream):
    deep = PIECE * DEEP
    cells = (OWN, ROWS, COLS, C)
    anywhere = pl.BlockSpec(memory_space=pl.ANY)
    outs = (
        jax.ShapeDtypeStruct(cells, BF),
        jax.ShapeDtypeStruct(cells, BF),
        jax.ShapeDtypeStruct((6 * C // ZS, C), F32),
    )
    kept = tuple(pltpu.VMEM(out.shape, out.dtype) for out in outs)
    inside = pl.BlockSpec(memory_space=pltpu.VMEM)
    parts = pl.pallas_call(
        kernel,
        out_shape=kept,
        in_specs=[anywhere] * 5,
        out_specs=(inside,) * 3,
        scratch_shapes=[
            pltpu.VMEM((2, 3, 3, C, C), BF),
            pltpu.VMEM((2, 3, C, C), BF),
            pltpu.VMEM((2, 3, 3, C, C), BF),
            pltpu.VMEM((2, 3, C, C), BF),
            pltpu.VMEM((2 * OWN, ROWS + 6, COLS, C), BF),
            pltpu.VMEM((OWN, ROWS + 4, COLS, C), BF),
            pltpu.VMEM((2 * OWN, ROWS + 4, COLS, C), BF),
            pltpu.VMEM((2 * OWN, ROWS, COLS, C), BF),
            pltpu.VMEM((OWN, ROWS, COLS, C), F32),
            pltpu.VMEM((OWN, ROWS + 2, COLS, C), F32),
            pltpu.VMEM((2 * OWN, ROWS + 2, COLS, C), BF),
            pltpu.VMEM((2 * OWN, ROWS, COLS, C), BF),
            pltpu.VMEM((OWN, ROWS + 2, COLS, C), BF),
            pltpu.VMEM((OWN, ROWS + 2, COLS, C), BF),
            pltpu.VMEM((OWN, ROWS + 2, COLS, C), F32),
            pltpu.VMEM((C, 2 * CELLS), BF),
            pltpu.VMEM((2, 3 * C, C), F32),
            pltpu.VMEM((2, CHIPS, deep, C), F32),
            pltpu.VMEM((2, CHIPS, deep, HALF), BF),
            pltpu.VMEM((2, CHIPS, deep, HALF), BF),
            pltpu.VMEM((2, CHIPS, deep, HALF), BF),
            pltpu.VMEM((2, CHIPS, deep, HALF), BF),
            pltpu.VMEM((ZS, 8, HALF), F32),
            pltpu.VMEM((ZS, 8, HALF), F32),
            pltpu.VMEM((8, HALF), F32),
            pltpu.VMEM((PLANE, 8, HALF), F32),
            pltpu.SMEM((1, FRAMES), jnp.int32),
            pltpu.SemaphoreType.DMA((6,)),
            pltpu.SemaphoreType.DMA((14,)),
            pltpu.SemaphoreType.DMA((14,)),
            pltpu.SemaphoreType.DMA((4,)),
            pltpu.SemaphoreType.DMA((4,)),
            pltpu.SemaphoreType.DMA((12,)),
            pltpu.SemaphoreType.REGULAR((3,)),
        ],
        compiler_params=pltpu.CompilerParams(
            collective_id=0, has_side_effects=True, vmem_limit_bytes=56 * 1024 * 1024
        ),
    )(
        segment_ids,
        clips.reshape(cells),
        spatial_weight.reshape(2, 3, 3, C, C),
        temporal_weight,
        upstream.reshape(cells),
    )
    parts = [pltpu.with_memory_space_constraint(part, pltpu.VMEM) for part in parts]
    grad, features, weight_grad = pl.pallas_call(
        finish,
        out_shape=outs,
        in_specs=[inside] * 3,
        out_specs=(anywhere,) * 3,
        scratch_shapes=[pltpu.SemaphoreType.DMA((3,))],
    )(*parts)
    return (grad.reshape(clips.shape), features.reshape(clips.shape), weight_grad)


def solution(mesh):
    return jax.shard_map(
        local,
        mesh=mesh,
        in_specs=(
            P("dp", "tm", "rows", None, None),
            P("dp", None),
            P(),
            P(),
            P("dp", "tm", "rows", None, None),
        ),
        out_specs=(
            P("dp", "tm", "rows", None, None),
            P("dp", "tm", "rows", None, None),
            P("rows", None),
        ),
        check_vma=False,
    )
```
